32 devices in a mesh: shot: 2 (over y), gy: 4 (over z), gx: 4 (over x, core).
Axes of the slice: x: 2, y: 2, z: 4, core: 2. Of those that a mesh axis runs over, the one named last changes fastest.
Arguments:
- pressure_now: float32 [128, 64, 512], P(('shot', 'gx'), 'gy'), parts along dimension 0, may hold values from -6 to 6
- pressure_old: float32 [128, 64, 512], P(('shot', 'gx'), 'gy'), parts along dimension 0, may hold values from -6 to 6
- classes: int32 [128, 64, 512], P(('shot', 'gx'), 'gy'), parts along dimension 0, may hold values from 0 to 15
- class_table: float32 [16], replicated, may hold values from 0.02 to 0.19
- wavelet: float32 [512], P('shot'), parts along dimension 0, may hold values from -12 to 12
- source_cells: int32 [8], P('shot'), parts along dimension 0, may hold values from 0 to 2097151
- samples: int32 [8], P('shot'), parts along dimension 0, may hold values from 0 to 255
Outputs:
- pressure_next: float32 [128, 64, 512], P(('shot', 'gx'), 'gy'), parts along dimension 0
- pressure_mid: float32 [128, 64, 512], P(('shot', 'gx'), 'gy'), parts along dimension 0
- snapshot_code: float32 [128, 64, 512], P(('shot', 'gx'), 'gy'), parts along dimension 0
The draws below stay inside these ranges and needn't reach their ends.
There are 2 independent parts, one for each index of `shot`. The reference program is written for one: setup_inputs(seed, part) draws one part's arguments, and reference() takes and returns one part's arrays. A program takes and returns all parts, laid end to end along the dimension named above; an argument that names none is the same for every part. Nothing has to cross between parts.
Inputs may be any that keep to these rules, and one draw needn't show every extreme that they name: `source_cells`: decoded as ix * 64 * 512 + iy * 512 + iz.
All inputs are finite; a program needn't handle non-finite values.
Results may differ from the reference program's by a relative error of at most 0.0003.
Values sent between devices are 32-bit elements; how exact they have to be, the bound alone decides.
A program may use at most 64 MiB of HBM per device.

```python
import math
import jax
import jax.numpy as jnp
from jax import lax

NZ = 512
NCLASS = 16
SHOTS = 4
NT = 256
NX = 64
NY = 64


def with_ends(values, own_key, smallest, high):
    spot = [jax.random.randint(jax.random.fold_in(own_key, axis), (), 0, length) for axis, length in enumerate(values.shape)]
    longest = values.shape.index(max(values.shape))
    beside = spot[:longest] + [(spot[longest] + 1) % values.shape[longest]] + spot[longest + 1:]
    return values.at[tuple(spot)].set(smallest).at[tuple(beside)].set(high)


def level_of(key, dims, split, smallest, top_value):
    factor_of, own = 1.0, jax.random.fold_in(key, 6)
    for axis_at, blocks in split:
        heights = jnp.exp(jax.random.uniform(jax.random.fold_in(own, axis_at), (blocks,), jnp.float32, smallest / len(split), top_value / len(split)))
        factor_of = factor_of * jnp.repeat(heights, dims[axis_at] // blocks).reshape([-1 if axis == axis_at else 1 for axis in range(len(dims))])
    return factor_of


def bell_draw(rng, extent, scale, most, split=(), dtype=jnp.bfloat16):
    drawn = scale * jax.random.normal(rng, extent, jnp.float32)
    if split:
        drawn = drawn * level_of(rng, extent, split, -0.22, 0.18)
    return jnp.clip(drawn, -most, most).astype(dtype)


def setup_inputs(seed: int = 0, part: int = 0) -> dict:
    streams_of = jax.random.split(jax.random.key(seed), 8)
    part_splits = jax.random.split(jax.random.fold_in(streams_of[7], part), 8)
    pressure_now = bell_draw(part_splits[0], (NX, NY, NZ), 1.0, 6.0, ((0, 4), (1, 4)), jnp.float32)
    pressure_old = bell_draw(part_splits[1], (NX, NY, NZ), 1.0, 6.0, ((0, 4), (1, 4)), jnp.float32)
    classes = with_ends(jax.random.randint(part_splits[2], (NX, NY, NZ), 0, NCLASS), jax.random.fold_in(part_splits[2], 1), 0, NCLASS - 1).astype(jnp.int32)
    class_table = jnp.clip(jnp.exp(jax.random.uniform(streams_of[3], (NCLASS,), jnp.float32, math.log(0.02), math.log(0.19))), 0.02, 0.19)
    wavelet = bell_draw(part_splits[4], (NT,), 3.0, 12.0, (), jnp.float32)
    source_cells = with_ends(jax.random.randint(part_splits[5], (SHOTS,), 0, NX * NY * NZ), jax.random.fold_in(part_splits[5], 1), 0, (NX * NY * NZ) - 1).astype(jnp.int32)
    samples = with_ends(jax.random.randint(part_splits[6], (SHOTS,), 0, NT), jax.random.fold_in(part_splits[6], 1), 0, NT - 1).astype(jnp.int32)
    return {"pressure_now": pressure_now, "pressure_old": pressure_old, "classes": classes, "class_table": class_table, "wavelet": wavelet, "source_cells": source_cells, "samples": samples}


STENCIL_WEIGHTS = (-205.0 / 72.0, 8.0 / 5.0, -1.0 / 5.0, 8.0 / 315.0, -1.0 / 560.0)
LIFT_ALPHA = -1.586134342
LIFT_BETA = -0.05298011854
LIFT_GAMMA = 0.8829110762
LIFT_DELTA = 0.4435068522
LIFT_SCALE = 1.149604398
DEAD_ZONE = 0.25
QUANT_STEP = 0.5


def laplace(extended):
    size_x = extended.shape[0] - 8
    size_y = extended.shape[1] - 8
    depth = extended.shape[2]
    depth_padded = jnp.pad(extended[:, 4:4 + size_y, :], ((0, 0), (0, 0), (4, 4)))
    center = extended[4:4 + size_x, 4:4 + size_y, :]
    summed = (3.0 * STENCIL_WEIGHTS[0]) * center
    for offset in range(1, 5):
        beside = extended[4 + offset:4 + offset + size_x, 4:4 + size_y, :] + extended[4 - offset:4 - offset + size_x, 4:4 + size_y, :]
        beside = beside + extended[4:4 + size_x, 4 + offset:4 + offset + size_y, :] + extended[4:4 + size_x, 4 - offset:4 - offset + size_y, :]
        beside = beside + depth_padded[4:4 + size_x, :, 4 + offset:4 + offset + depth] + depth_padded[4:4 + size_x, :, 4 - offset:4 - offset + depth]
        summed = summed + STENCIL_WEIGHTS[offset] * beside
    return summed


def cut_range(field, start, limit, along):
    return lax.slice_in_dim(field, start, limit, 1, along)


def lift_core(padded, along):
    length = padded.shape[along]
    even = lax.slice_in_dim(padded, 0, length, 2, along)
    odd = lax.slice_in_dim(padded, 1, length, 2, along)
    half = even.shape[along]
    odd_one = cut_range(odd, 0, half - 1, along) + LIFT_ALPHA * (cut_range(even, 0, half - 1, along) + cut_range(even, 1, half, along))
    even_one = cut_range(even, 1, half - 1, along) + LIFT_BETA * (cut_range(odd_one, 0, half - 2, along) + cut_range(odd_one, 1, half - 1, along))
    odd_two = cut_range(odd_one, 1, half - 2, along) + LIFT_GAMMA * (cut_range(even_one, 0, half - 3, along) + cut_range(even_one, 1, half - 2, along))
    even_two = cut_range(even_one, 1, half - 3, along) + LIFT_DELTA * (cut_range(odd_two, 0, half - 4, along) + cut_range(odd_two, 1, half - 3, along))
    low_band = even_two / LIFT_SCALE
    high_band = cut_range(odd_two, 1, half - 3, along) * LIFT_SCALE
    joined = jnp.stack([low_band, high_band], along + 1)
    shape = low_band.shape[:along] + (2 * low_band.shape[along],) + low_band.shape[along + 1:]
    return joined.reshape(shape)


def reflect_lift(field, along):
    widths = [(0, 0)] * field.ndim
    widths[along] = (4, 4)
    return lift_core(jnp.pad(field, widths, mode="reflect"), along)


def quantize(values):
    return jnp.sign(values) * jnp.maximum(jnp.abs(values) - DEAD_ZONE, 0.0) / QUANT_STEP


def source_field(source_cells, samples, wavelet, step_index):
    cell_x = source_cells // (NY * NZ)
    cell_y = (source_cells // NZ) % NY
    cell_z = source_cells % NZ
    amplitude = wavelet[(samples + step_index) % NT]
    return jnp.zeros((NX, NY, NZ), jnp.float32).at[cell_x, cell_y, cell_z].add(amplitude)


def advance(field, older, courant, source):
    extended = jnp.pad(field, ((4, 4), (4, 4), (0, 0)))
    return 2.0 * field - older + courant * laplace(extended) + source


def reference(pressure_now, pressure_old, classes, class_table, wavelet, source_cells, samples):
    courant = class_table[classes]
    pressure_mid = advance(pressure_now, pressure_old, courant, source_field(source_cells, samples, wavelet, 0))
    pressure_next = advance(pressure_mid, pressure_now, courant, source_field(source_cells, samples, wavelet, 1))
    lifted = reflect_lift(pressure_next, 2)
    lifted = reflect_lift(lifted, 0)
    lifted = reflect_lift(lifted, 1)
    return pressure_next, pressure_mid, quantize(lifted)
```

```python
import functools

import jax
import jax.numpy as jnp
import ml_dtypes
import numpy as np
from jax import lax
from jax.experimental import pallas as pl
from jax.experimental.pallas import tpu as pltpu
from jax.sharding import PartitionSpec as P

STENCIL_WEIGHTS = (-205.0 / 72.0, 8.0 / 5.0, -1.0 / 5.0, 8.0 / 315.0, -1.0 / 560.0)
LIFT_ALPHA = -1.586134342
LIFT_BETA = -0.05298011854
LIFT_GAMMA = 0.8829110762
LIFT_DELTA = 0.4435068522
LIFT_SCALE = 1.149604398
DEAD_ZONE = 0.25
QUANT_STEP = 0.5
W = 4
MESH = pl.DeviceIdType.MESH


def lift_matrix(size):
    field = np.eye(size + 2 * W)
    even, odd = field[0::2], field[1::2]
    odd = odd[:-1] + LIFT_ALPHA * (even[:-1] + even[1:])
    even = even[1:-1] + LIFT_BETA * (odd[:-1] + odd[1:])
    odd = odd[1:-1] + LIFT_GAMMA * (even[:-1] + even[1:])
    even = even[1:-1] + LIFT_DELTA * (odd[:-1] + odd[1:])
    out = np.zeros((size, size + 2 * W))
    out[0::2] = even / LIFT_SCALE
    out[1::2] = odd[1:] * LIFT_SCALE
    return out


def reflected(matrix, first, last):
    size = matrix.shape[0]
    out = matrix.copy()
    for step in range(1, W + 1):
        if first:
            out[:, W + step] += out[:, W - step]
            out[:, W - step] = 0.0
        if last:
            out[:, W + size - 1 - step] += out[:, W + size - 1 + step]
            out[:, W + size - 1 + step] = 0.0
    return out


def halves(matrix):
    wide = np.asarray(matrix, np.float32)
    high = wide.astype(ml_dtypes.bfloat16)
    low = (wide - high.astype(np.float32)).astype(ml_dtypes.bfloat16)
    return np.stack([high, low], axis=-3)


def halo_cells(rows_x, rows_y):
    low, x_high, y_high = range(-W, 0), range(rows_x, rows_x + W), range(rows_y, rows_y + W)
    cells = [(x, y) for x in low for y in range(rows_y)]
    cells += [(x, y) for x in x_high for y in range(rows_y)]
    cells += [(x, y) for x in range(rows_x) for y in low]
    cells += [(x, y) for x in range(rows_x) for y in y_high]
    faces = len(cells)
    for side_x in (low, x_high):
        for side_y in (low, y_high):
            cells += [(x, y) for x in side_x for y in side_y]
    return cells, faces


@functools.lru_cache(None)
def tables(rows_x, rows_y, depth):
    cells, faces = halo_cells(rows_x, rows_y)
    own = [(x, y) for x in range(rows_x) for y in range(rows_y)]
    everywhere = np.array(own + cells)
    target = np.array(own)
    gap_x = np.abs(target[:, None, 0] - everywhere[None, :, 0])
    gap_y = np.abs(target[:, None, 1] - everywhere[None, :, 1])
    weights = np.array(list(STENCIL_WEIGHTS) + [0.0])
    star = np.where(gap_y == 0, weights[np.minimum(gap_x, W + 1)], 0.0)
    star = star + np.where(gap_x == 0, weights[np.minimum(gap_y, W + 1)], 0.0)
    star = star[:, : len(own) + faces]
    spot = np.arange(depth)
    along = weights[np.minimum(np.abs(spot[:, None] - spot[None, :]), W + 1)]
    depth_lift = reflected(lift_matrix(depth), True, True)[:, W : W + depth].T
    kinds = ((False, False), (True, False), (False, True))
    lifts = []
    for kind_x in kinds:
        for kind_y in kinds:
            by_x = reflected(lift_matrix(rows_x), *kind_x)[:, everywhere[:, 0] + W]
            by_y = reflected(lift_matrix(rows_y), *kind_y)[:, everywhere[:, 1] + W]
            lifts.append(by_x[target[:, 0]] * by_y[target[:, 1]])
    lifts = np.stack(lifts)
    spare = -lifts.shape[2] % 128
    lifts = np.pad(lifts, ((0, 0), (0, 0), (0, spare)))
    depth_both = np.concatenate([halves(along), halves(depth_lift)])
    return halves(star), depth_both, halves(lifts)


def split(values):
    high = values.astype(jnp.bfloat16)
    return high, (values - high.astype(jnp.float32)).astype(jnp.bfloat16)


def product(left, right):
    dot = functools.partial(jnp.dot, preferred_element_type=jnp.float32)
    return dot(left[0], right[0]) + (dot(left[0], right[1]) + dot(left[1], right[0]))


def choose(classes, entries, bit):
    if len(entries) == 1:
        return entries[0]
    half = len(entries) // 2
    low = choose(classes, entries[:half], bit // 2)
    high = choose(classes, entries[half:], bit // 2)
    return jnp.where((classes & bit) != 0, high, low)


def kernel(
    rows_x, rows_y,
    cells_ref, samples_ref, wave_ref, table_ref,
    now_hbm, old_hbm, classes_hbm, star_hbm, along_hbm, lift_hbm,
    next_hbm, mid_hbm, code_hbm,
    now, old, classes, star, along, lift,
    courant, mid, later, acc, packed, halo_a, halo_b, halo_c,
    local_sem, out_sem, send_sem, recv_sem,
):
    depth = now.shape[1]
    size = rows_x * rows_y
    face_x, face_y, corner = W * rows_y, W * rows_x, W * W
    faces = 2 * face_x + 2 * face_y
    at_x, at_y = lax.axis_index("gx"), lax.axis_index("gy")
    count_x, count_y = lax.axis_size("gx"), lax.axis_size("gy")
    shot = lax.axis_index("shot")
    low_x, high_x = at_x > 0, at_x < count_x - 1
    low_y, high_y = at_y > 0, at_y < count_y - 1
    kind_x = jnp.where(low_x, jnp.where(high_x, 0, 2), 1)
    kind_y = jnp.where(low_y, jnp.where(high_y, 0, 2), 1)

    pulls = [
        pltpu.make_async_copy(src, dst, local_sem.at[i])
        for i, (src, dst) in enumerate(
            [
                (now_hbm, now), (classes_hbm, classes), (old_hbm, old),
                (star_hbm, star), (along_hbm, along),
                (lift_hbm.at[kind_x * 3 + kind_y], lift),
            ]
        )
    ]
    for pull in pulls:
        pull.start()

    steps = ((-1, low_x, low_y), (1, high_x, high_y))
    partners = [(dx, 0, has) for dx, has, _ in steps] + [(0, dy, has) for dy, _, has in steps]
    partners += [
        (dx, dy, jnp.logical_and(has_x, has_y)) for dx, has_x, _ in steps for dy, _, has_y in steps
    ]

    def device(dx, dy):
        return {"shot": shot, "gy": at_y + dy, "gx": at_x + dx}

    barrier = pltpu.get_barrier_semaphore()
    for dx, dy, has in partners:
        @pl.when(has)
        def _(dx=dx, dy=dy):
            pl.semaphore_signal(barrier, inc=1, device_id=device(dx, dy), device_id_type=MESH)

    def pack(source, where):
        for x in range(0, rows_x, 2):
            first, second = x * rows_y, (x + 1) * rows_y
            packed[where, 0, x * W : (x + 2) * W, :] = jnp.concatenate(
                [source[first : first + W, :], source[second : second + W, :]], axis=0
            )
            packed[where, 1, x * W : (x + 2) * W, :] = jnp.concatenate(
                [source[first + rows_y - W : second, :],
                 source[second + rows_y - W : second + rows_y, :]], axis=0
            )

    slots = [(0, face_x), (face_x, face_x), (2 * face_x, face_y), (2 * face_x + face_y, face_y)]
    slots += [(faces + i * corner, corner) for i in range(4)]

    def exchange(source, halo, where, base, with_corners):
        ends = [
            source.at[pl.ds(0, face_x)],
            source.at[pl.ds(size - face_x, face_x)],
            packed.at[where, 0],
            packed.at[where, 1],
            packed.at[where, 0, pl.ds(0, corner)],
            packed.at[where, 1, pl.ds(0, corner)],
            packed.at[where, 0, pl.ds(face_y - corner, corner)],
            packed.at[where, 1, pl.ds(face_y - corner, corner)],
        ]
        opposite = [1, 0, 3, 2, 7, 6, 5, 4]
        sends, arrivals = [], []
        for i in range(8 if with_corners else 4):
            dx, dy, has = partners[i]
            for to, found in ((opposite[i], sends), (i, arrivals)):
                start, length = slots[to]
                found.append((has, pltpu.make_async_remote_copy(
                    src_ref=ends[i],
                    dst_ref=halo.at[pl.ds(start, length)],
                    send_sem=send_sem.at[base + i],
                    recv_sem=recv_sem.at[base + to],
                    device_id=device(dx, dy),
                    device_id_type=MESH,
                )))
        return sends, arrivals

    def each(copies, act):
        for has, copy in copies:
            @pl.when(has)
            def _(copy=copy):
                act(copy)

    start = lambda copy: copy.start()
    landed = lambda copy: copy.wait_recv()
    sent = lambda copy: copy.wait_send()

    first_sends, first_lands = exchange(now, halo_a, 0, 0, False)
    second_sends, second_lands = exchange(mid, halo_b, 1, 4, False)
    third_sends, third_lands = exchange(later, halo_c, 2, 8, True)

    for halo, lands in ((halo_a, first_lands), (halo_b, second_lands), (halo_c, third_lands)):
        for i, (has, _) in enumerate(lands):
            begin, length = slots[i]

            @pl.when(jnp.logical_not(has))
            def _(halo=halo, begin=begin, length=length):
                halo[begin : begin + length, :] = jnp.zeros((length, depth), jnp.float32)
    tail = faces + 4 * corner
    if halo_c.shape[0] > tail:
        halo_c[tail:, :] = jnp.zeros((halo_c.shape[0] - tail, depth), jnp.float32)

    pulls[0].wait()
    pack(now, 0)
    near_x = low_x.astype(jnp.int32) + high_x.astype(jnp.int32)
    near_y = low_y.astype(jnp.int32) + high_y.astype(jnp.int32)
    pl.semaphore_wait(barrier, near_x + near_y + near_x * near_y)
    each(first_sends[2:], start)
    each(first_sends[:2], start)

    wave_len = wave_ref.shape[0]
    all_y = rows_y * count_y
    shots = []
    for s in range(cells_ref.shape[0]):
        cell, sample = cells_ref[s], samples_ref[s]
        cell_x = lax.div(cell, all_y * depth) - at_x * rows_x
        cell_y = lax.rem(lax.div(cell, depth), all_y) - at_y * rows_y
        here = (cell_x >= 0) & (cell_x < rows_x) & (cell_y >= 0) & (cell_y < rows_y)
        spot = jnp.where(here, (cell_x * rows_y + cell_y) * depth + lax.rem(cell, depth), -1)
        following = jnp.where(sample + 1 >= wave_len, 0, sample + 1)
        shots.append((spot, wave_ref[sample], wave_ref[following]))
    entries = [table_ref[i] for i in range(table_ref.shape[0])]
    while len(entries) & (len(entries) - 1):
        entries.append(entries[-1])
    pulls[1].wait()
    pulls[2].wait()

    def plane(x, carry):
        rows = pl.ds(pl.multiple_of(x * rows_y, rows_y), rows_y)
        courant[rows, :] = jnp.broadcast_to(
            choose(classes[rows, :], entries, len(entries) // 2), (rows_y, depth)
        )
        place = lax.broadcasted_iota(jnp.int32, (rows_y, depth), 0) * depth
        place = place + lax.broadcasted_iota(jnp.int32, (rows_y, depth), 1)
        here = now[rows, :]
        base_a = 2.0 * here - old[rows, :]
        base_b = -here
        for spot, amp_a, amp_b in shots:
            hit = place == spot - x * (rows_y * depth)
            base_a = base_a + jnp.where(hit, amp_a, 0.0)
            base_b = base_b + jnp.where(hit, amp_b, 0.0)
        old[rows, :] = base_a
        later[rows, :] = base_b
        return carry

    lax.fori_loop(0, rows_x, plane, 0)
    pulls[3].wait()
    pulls[4].wait()

    def inner(field):
        both = split(field[...])
        own = [star[0, :, :size], star[1, :, :size]]
        acc[...] = product(own, both) + product(both, (along[0], along[1]))

    def outer(halo):
        return product([star[0, :, size:], star[1, :, size:]], split(halo[...]))

    inner(now)
    each(first_lands, landed)
    mid[...] = old[...] + courant[...] * (acc[...] + outer(halo_a))
    each(second_sends[:2], start)
    pack(mid, 1)
    each(second_sends[2:], start)
    mid_out = pltpu.make_async_copy(mid, mid_hbm, out_sem.at[0])
    mid_out.start()

    later[...] = later[...] + 2.0 * mid[...]
    inner(mid)
    each(second_lands, landed)
    later[...] = later[...] + courant[...] * (acc[...] + outer(halo_b))
    each(third_sends[:2], start)
    pack(later, 2)
    each(third_sends[2:], start)
    next_out = pltpu.make_async_copy(later, next_hbm, out_sem.at[1])
    next_out.start()

    pulls[5].wait()
    acc[...] = product([lift[0, :, :size], lift[1, :, :size]], split(later[...]))
    each(third_lands, landed)
    lifted = acc[...] + product([lift[0, :, size:], lift[1, :, size:]], split(halo_c[...]))
    lifted = product(split(lifted), (along[2], along[3]))
    shrunk = jnp.maximum(jnp.abs(lifted) - DEAD_ZONE, 0.0) / QUANT_STEP
    acc[...] = jnp.where(lifted < 0.0, -shrunk, shrunk)
    code_out = pltpu.make_async_copy(acc, code_hbm, out_sem.at[2])
    code_out.start()
    each(first_sends, sent)
    each(second_sends, sent)
    each(third_sends, sent)
    mid_out.wait()
    next_out.wait()
    code_out.wait()


def shards(pressure_now, pressure_old, classes, class_table, wavelet, source_cells, samples):
    rows_x, rows_y, depth = pressure_now.shape
    size = rows_x * rows_y
    flat = (size, depth)
    star, along, lift = tables(rows_x, rows_y, depth)
    halo_rows = star.shape[2] - size
    wide_rows = lift.shape[3] - size
    face_y = W * rows_x
    any_spec = pl.BlockSpec(memory_space=pl.ANY)
    smem = pl.BlockSpec(memory_space=pltpu.SMEM)
    f32 = jnp.float32
    out = jax.ShapeDtypeStruct(flat, f32)
    results = pl.pallas_call(
        functools.partial(kernel, rows_x, rows_y),
        out_shape=(out, out, out),
        in_specs=[smem] * 4 + [any_spec] * 6,
        out_specs=(any_spec,) * 3,
        scratch_shapes=[
            pltpu.VMEM(flat, f32),
            pltpu.VMEM(flat, f32),
            pltpu.VMEM(flat, jnp.int32),
            pltpu.VMEM(star.shape, jnp.bfloat16),
            pltpu.VMEM(along.shape, jnp.bfloat16),
            pltpu.VMEM(lift.shape[1:], jnp.bfloat16),
            pltpu.VMEM(flat, f32),
            pltpu.VMEM(flat, f32),
            pltpu.VMEM(flat, f32),
            pltpu.VMEM(flat, f32),
            pltpu.VMEM((3, 2, face_y, depth), f32),
            pltpu.VMEM((halo_rows, depth), f32),
            pltpu.VMEM((halo_rows, depth), f32),
            pltpu.VMEM((wide_rows, depth), f32),
            pltpu.SemaphoreType.DMA((6,)),
            pltpu.SemaphoreType.DMA((3,)),
            pltpu.SemaphoreType.DMA((16,)),
            pltpu.SemaphoreType.DMA((16,)),
        ],
        compiler_params=pltpu.CompilerParams(
            collective_id=0, has_side_effects=True, vmem_limit_bytes=40 * 1024 * 1024
        ),
    )(
        source_cells, samples, wavelet, class_table,
        pressure_now.reshape(flat), pressure_old.reshape(flat), classes.reshape(flat),
        jnp.asarray(star), jnp.asarray(along), jnp.asarray(lift),
    )
    return tuple(result.reshape(pressure_now.shape) for result in results)


def solution(mesh):
    block = P(("shot", "gx"), "gy", None)
    return jax.shard_map(
        shards,
        mesh=mesh,
        in_specs=(block, block, block, P(), P("shot"), P("shot"), P("shot")),
        out_specs=(block, block, block),
        check_vma=False,
    )
```

```python
import functools

import jax
import jax.numpy as jnp
import ml_dtypes
import numpy as np
from jax import lax
from jax.experimental import pallas as pl
from jax.experimental.pallas import tpu as pltpu
from jax.sharding import PartitionSpec as P

STENCIL_WEIGHTS = (-205.0 / 72.0, 8.0 / 5.0, -1.0 / 5.0, 8.0 / 315.0, -1.0 / 560.0)
LIFT_ALPHA = -1.586134342
LIFT_BETA = -0.05298011854
LIFT_GAMMA = 0.8829110762
LIFT_DELTA = 0.4435068522
LIFT_SCALE = 1.149604398
DEAD_ZONE = 0.25
QUANT_STEP = 0.5
W = 4
MESH = pl.DeviceIdType.MESH
VMEM_BYTES = 62 * 1024 * 1024


def lift_matrix(size):
    field = np.eye(size + 2 * W)
    even, odd = field[0::2], field[1::2]
    odd = odd[:-1] + LIFT_ALPHA * (even[:-1] + even[1:])
    even = even[1:-1] + LIFT_BETA * (odd[:-1] + odd[1:])
    odd = odd[1:-1] + LIFT_GAMMA * (even[:-1] + even[1:])
    even = even[1:-1] + LIFT_DELTA * (odd[:-1] + odd[1:])
    out = np.zeros((size, size + 2 * W))
    out[0::2] = even / LIFT_SCALE
    out[1::2] = odd[1:] * LIFT_SCALE
    return out


def reflected(matrix, first, last):
    size = matrix.shape[0]
    out = matrix.copy()
    for step in range(1, W + 1):
        if first:
            out[:, W + step] += out[:, W - step]
            out[:, W - step] = 0.0
        if last:
            out[:, W + size - 1 - step] += out[:, W + size - 1 + step]
            out[:, W + size - 1 + step] = 0.0
    return out


def halves(matrix):
    wide = np.asarray(matrix, np.float32)
    high = wide.astype(ml_dtypes.bfloat16)
    low = (wide - high.astype(np.float32)).astype(ml_dtypes.bfloat16)
    return np.stack([high, low], axis=-3)


def halo_cells(rows_x, rows_y):
    low, x_high, y_high = range(-W, 0), range(rows_x, rows_x + W), range(rows_y, rows_y + W)
    cells = [(x, y) for x in low for y in range(rows_y)]
    cells += [(x, y) for x in x_high for y in range(rows_y)]
    cells += [(x, y) for x in range(rows_x) for y in low]
    cells += [(x, y) for x in range(rows_x) for y in y_high]
    faces = len(cells)
    for side_x in (low, x_high):
        for side_y in (low, y_high):
            cells += [(x, y) for x in side_x for y in side_y]
    return cells, faces


@functools.lru_cache(None)
def tables(rows_x, rows_y, depth):
    cells, faces = halo_cells(rows_x, rows_y)
    own = [(x, y) for x in range(rows_x) for y in range(rows_y)]
    everywhere = np.array(own + cells)
    target = np.array(own)
    gap_x = np.abs(target[:, None, 0] - everywhere[None, :, 0])
    gap_y = np.abs(target[:, None, 1] - everywhere[None, :, 1])
    weights = np.array(list(STENCIL_WEIGHTS) + [0.0])
    star = np.where(gap_y == 0, weights[np.minimum(gap_x, W + 1)], 0.0)
    star = star + np.where(gap_x == 0, weights[np.minimum(gap_y, W + 1)], 0.0)
    star = star[:, : len(own) + faces]
    spot = np.arange(depth)
    along = weights[np.minimum(np.abs(spot[:, None] - spot[None, :]), W + 1)]
    depth_lift = reflected(lift_matrix(depth), True, True)[:, W : W + depth].T
    kinds = ((False, False), (True, False), (False, True))
    lifts = []
    for kind_x in kinds:
        for kind_y in kinds:
            by_x = reflected(lift_matrix(rows_x), *kind_x)[:, everywhere[:, 0] + W]
            by_y = reflected(lift_matrix(rows_y), *kind_y)[:, everywhere[:, 1] + W]
            lifts.append(by_x[target[:, 0]] * by_y[target[:, 1]])
    lifts = np.stack(lifts)
    spare = -lifts.shape[2] % 128
    lifts = np.pad(lifts, ((0, 0), (0, 0), (0, spare)))
    depth_both = np.concatenate([halves(along), halves(depth_lift)])
    return halves(star), depth_both, halves(lifts)


def split(values):
    high = values.astype(jnp.bfloat16)
    return high, (values - high.astype(jnp.float32)).astype(jnp.bfloat16)


def product(left, right):
    dot = functools.partial(jnp.dot, preferred_element_type=jnp.float32)
    return dot(left[0], right[0]) + (dot(left[0], right[1]) + dot(left[1], right[0]))


def choose(classes, entries, bit):
    if len(entries) == 1:
        return entries[0]
    half = len(entries) // 2
    low = choose(classes, entries[:half], bit // 2)
    high = choose(classes, entries[half:], bit // 2)
    return jnp.where((classes & bit) != 0, high, low)


def kernel(
    rows_x, rows_y,
    cells_hbm, samples_hbm, wave_hbm, table_hbm,
    now_hbm, old_hbm, classes_hbm, star_hbm, along_hbm, lift_hbm,
    next_hbm, mid_hbm, code_hbm,
    cells_ref, samples_ref, wave_ref, table_ref,
    now, old, classes, star, along, lift,
    courant, mid, later, acc, packed, halo_a, halo_b, halo_c,
    local_sem, out_sem, send_sem, recv_sem,
):
    depth = now.shape[1]
    size = rows_x * rows_y
    face_x, face_y, corner = W * rows_y, W * rows_x, W * W
    faces = 2 * face_x + 2 * face_y
    at_x, at_y = lax.axis_index("gx"), lax.axis_index("gy")
    count_x, count_y = lax.axis_size("gx"), lax.axis_size("gy")
    shot = lax.axis_index("shot")
    low_x, high_x = at_x > 0, at_x < count_x - 1
    low_y, high_y = at_y > 0, at_y < count_y - 1
    kind_x = jnp.where(low_x, jnp.where(high_x, 0, 2), 1)
    kind_y = jnp.where(low_y, jnp.where(high_y, 0, 2), 1)

    pulls = [
        pltpu.make_async_copy(src, dst, local_sem.at[i])
        for i, (src, dst) in enumerate(
            [
                (now_hbm, now), (classes_hbm, classes), (old_hbm, old),
                (star_hbm, star), (along_hbm, along),
                (lift_hbm.at[kind_x * 3 + kind_y], lift),
                (cells_hbm, cells_ref), (samples_hbm, samples_ref),
                (wave_hbm, wave_ref), (table_hbm, table_ref),
            ]
        )
    ]
    for pull in pulls:
        pull.start()

    steps = ((-1, low_x, low_y), (1, high_x, high_y))
    partners = [(dx, 0, has) for dx, has, _ in steps] + [(0, dy, has) for dy, _, has in steps]
    partners += [
        (dx, dy, jnp.logical_and(has_x, has_y)) for dx, has_x, _ in steps for dy, _, has_y in steps
    ]

    def device(dx, dy):
        return {"shot": shot, "gy": at_y + dy, "gx": at_x + dx}

    barrier = pltpu.get_barrier_semaphore()
    for dx, dy, has in partners:
        @pl.when(has)
        def _(dx=dx, dy=dy):
            pl.semaphore_signal(barrier, inc=1, device_id=device(dx, dy), device_id_type=MESH)

    def pack(source, where):
        for x in range(0, rows_x, 2):
            first, second = x * rows_y, (x + 1) * rows_y
            packed[where, 0, x * W : (x + 2) * W, :] = jnp.concatenate(
                [source[first : first + W, :], source[second : second + W, :]], axis=0
            )
            packed[where, 1, x * W : (x + 2) * W, :] = jnp.concatenate(
                [source[first + rows_y - W : second, :],
                 source[second + rows_y - W : second + rows_y, :]], axis=0
            )

    slots = [(0, face_x), (face_x, face_x), (2 * face_x, face_y), (2 * face_x + face_y, face_y)]
    slots += [(faces + i * corner, corner) for i in range(4)]

    def exchange(source, halo, where, base, with_corners):
        ends = [
            source.at[pl.ds(0, face_x)],
            source.at[pl.ds(size - face_x, face_x)],
            packed.at[where, 0],
            packed.at[where, 1],
            packed.at[where, 0, pl.ds(0, corner)],
            packed.at[where, 1, pl.ds(0, corner)],
            packed.at[where, 0, pl.ds(face_y - corner, corner)],
            packed.at[where, 1, pl.ds(face_y - corner, corner)],
        ]
        opposite = [1, 0, 3, 2, 7, 6, 5, 4]
        sends, arrivals = [], []
        for i in range(8 if with_corners else 4):
            dx, dy, has = partners[i]
            for to, found in ((opposite[i], sends), (i, arrivals)):
                start, length = slots[to]
                found.append((has, pltpu.make_async_remote_copy(
                    src_ref=ends[i],
                    dst_ref=halo.at[pl.ds(start, length)],
                    send_sem=send_sem.at[base + i],
                    recv_sem=recv_sem.at[base + to],
                    device_id=device(dx, dy),
                    device_id_type=MESH,
                )))
        return sends, arrivals

    def each(copies, act):
        for has, copy in copies:
            @pl.when(has)
            def _(copy=copy):
                act(copy)

    start = lambda copy: copy.start()
    landed = lambda copy: copy.wait_recv()
    sent = lambda copy: copy.wait_send()

    first_sends, first_lands = exchange(now, halo_a, 0, 0, False)
    second_sends, second_lands = exchange(mid, halo_b, 1, 4, False)
    third_sends, third_lands = exchange(later, halo_c, 2, 8, True)

    for halo, lands in ((halo_a, first_lands), (halo_b, second_lands), (halo_c, third_lands)):
        for i, (has, _) in enumerate(lands):
            begin, length = slots[i]

            @pl.when(jnp.logical_not(has))
            def _(halo=halo, begin=begin, length=length):
                halo[begin : begin + length, :] = jnp.zeros((length, depth), jnp.float32)
    tail = faces + 4 * corner
    if halo_c.shape[0] > tail:
        halo_c[tail:, :] = jnp.zeros((halo_c.shape[0] - tail, depth), jnp.float32)

    pulls[0].wait()
    pack(now, 0)
    near_x = low_x.astype(jnp.int32) + high_x.astype(jnp.int32)
    near_y = low_y.astype(jnp.int32) + high_y.astype(jnp.int32)
    pl.semaphore_wait(barrier, near_x + near_y + near_x * near_y)
    each(first_sends[2:], start)
    each(first_sends[:2], start)

    for pull in pulls[6:]:
        pull.wait()
    wave_len = wave_ref.shape[0]
    all_y = rows_y * count_y
    shots = []
    for s in range(cells_ref.shape[0]):
        cell, sample = cells_ref[s], samples_ref[s]
        cell_x = lax.div(cell, all_y * depth) - at_x * rows_x
        cell_y = lax.rem(lax.div(cell, depth), all_y) - at_y * rows_y
        here = (cell_x >= 0) & (cell_x < rows_x) & (cell_y >= 0) & (cell_y < rows_y)
        spot = jnp.where(here, (cell_x * rows_y + cell_y) * depth + lax.rem(cell, depth), -1)
        following = jnp.where(sample + 1 >= wave_len, 0, sample + 1)
        shots.append((spot, wave_ref[sample], wave_ref[following]))
    entries = [table_ref[i] for i in range(table_ref.shape[0])]
    while len(entries) & (len(entries) - 1):
        entries.append(entries[-1])
    pulls[1].wait()
    pulls[2].wait()

    def plane(x, carry):
        rows = pl.ds(pl.multiple_of(x * rows_y, rows_y), rows_y)
        courant[rows, :] = jnp.broadcast_to(
            choose(classes[rows, :], entries, len(entries) // 2), (rows_y, depth)
        )
        place = lax.broadcasted_iota(jnp.int32, (rows_y, depth), 0) * depth
        place = place + lax.broadcasted_iota(jnp.int32, (rows_y, depth), 1)
        here = now[rows, :]
        base_a = 2.0 * here - old[rows, :]
        base_b = -here
        for spot, amp_a, amp_b in shots:
            hit = place == spot - x * (rows_y * depth)
            base_a = base_a + jnp.where(hit, amp_a, 0.0)
            base_b = base_b + jnp.where(hit, amp_b, 0.0)
        old[rows, :] = base_a
        later[rows, :] = base_b
        return carry

    lax.fori_loop(0, rows_x, plane, 0)
    pulls[3].wait()
    pulls[4].wait()

    def inner(field):
        both = split(field[...])
        own = [star[0, :, :size], star[1, :, :size]]
        acc[...] = product(own, both) + product(both, (along[0], along[1]))

    def outer(halo):
        return product([star[0, :, size:], star[1, :, size:]], split(halo[...]))

    inner(now)
    each(first_lands, landed)
    mid[...] = old[...] + courant[...] * (acc[...] + outer(halo_a))
    each(second_sends[:2], start)
    pack(mid, 1)
    each(second_sends[2:], start)
    mid_out = pltpu.make_async_copy(mid, mid_hbm, out_sem.at[0])
    mid_out.start()

    later[...] = later[...] + 2.0 * mid[...]
    inner(mid)
    each(second_lands, landed)
    later[...] = later[...] + courant[...] * (acc[...] + outer(halo_b))
    each(third_sends[:2], start)
    pack(later, 2)
    each(third_sends[2:], start)
    next_out = pltpu.make_async_copy(later, next_hbm, out_sem.at[1])
    next_out.start()

    pulls[5].wait()
    acc[...] = product([lift[0, :, :size], lift[1, :, :size]], split(later[...]))
    each(third_lands, landed)
    lifted = acc[...] + product([lift[0, :, size:], lift[1, :, size:]], split(halo_c[...]))
    lifted = product(split(lifted), (along[2], along[3]))
    shrunk = jnp.maximum(jnp.abs(lifted) - DEAD_ZONE, 0.0) / QUANT_STEP
    acc[...] = jnp.where(lifted < 0.0, -shrunk, shrunk)
    code_out = pltpu.make_async_copy(acc, code_hbm, out_sem.at[2])
    code_out.start()
    each(first_sends, sent)
    each(second_sends, sent)
    each(third_sends, sent)
    mid_out.wait()
    next_out.wait()
    code_out.wait()


def put_out(*refs):
    sources, targets, sems = refs[:3], refs[3:6], refs[6]
    copies = [pltpu.make_async_copy(sources[i], targets[i], sems.at[i]) for i in range(3)]
    for copy in copies:
        copy.start()
    for copy in copies:
        copy.wait()


def shards(pressure_now, pressure_old, classes, class_table, wavelet, source_cells, samples):
    rows_x, rows_y, depth = pressure_now.shape
    size = rows_x * rows_y
    flat = (size, depth)
    star, along, lift = tables(rows_x, rows_y, depth)
    halo_rows = star.shape[2] - size
    wide_rows = lift.shape[3] - size
    face_y = W * rows_x
    hbm = pl.BlockSpec(memory_space=pltpu.HBM)
    f32 = jnp.float32
    out = jax.ShapeDtypeStruct(flat, f32)
    results = pl.pallas_call(
        functools.partial(kernel, rows_x, rows_y),
        out_shape=(out, out, out),
        in_specs=[hbm] * 10,
        out_specs=(hbm,) * 3,
        scratch_shapes=[
            pltpu.SMEM(source_cells.shape, jnp.int32),
            pltpu.SMEM(samples.shape, jnp.int32),
            pltpu.SMEM(wavelet.shape, f32),
            pltpu.SMEM(class_table.shape, f32),
            pltpu.VMEM(flat, f32),
            pltpu.VMEM(flat, f32),
            pltpu.VMEM(flat, jnp.int32),
            pltpu.VMEM(star.shape, jnp.bfloat16),
            pltpu.VMEM(along.shape, jnp.bfloat16),
            pltpu.VMEM(lift.shape[1:], jnp.bfloat16),
            pltpu.VMEM(flat, f32),
            pltpu.VMEM(flat, f32),
            pltpu.VMEM(flat, f32),
            pltpu.VMEM(flat, f32),
            pltpu.VMEM((3, 2, face_y, depth), f32),
            pltpu.VMEM((halo_rows, depth), f32),
            pltpu.VMEM((halo_rows, depth), f32),
            pltpu.VMEM((wide_rows, depth), f32),
            pltpu.SemaphoreType.DMA((10,)),
            pltpu.SemaphoreType.DMA((3,)),
            pltpu.SemaphoreType.DMA((16,)),
            pltpu.SemaphoreType.DMA((16,)),
        ],
        compiler_params=pltpu.CompilerParams(
            collective_id=0, has_side_effects=True, vmem_limit_bytes=VMEM_BYTES
        ),
    )(
        source_cells, samples, wavelet, class_table,
        pressure_now.reshape(flat), pressure_old.reshape(flat), classes.reshape(flat),
        jnp.asarray(star), jnp.asarray(along), jnp.asarray(lift),
    )
    results = pl.pallas_call(
        put_out,
        out_shape=(out, out, out),
        in_specs=[hbm] * 3,
        out_specs=(hbm,) * 3,
        scratch_shapes=[pltpu.SemaphoreType.DMA((3,))],
        compiler_params=pltpu.CompilerParams(vmem_limit_bytes=VMEM_BYTES),
    )(*results)
    return tuple(result.reshape(pressure_now.shape) for result in results)


def solution(mesh):
    block = P(("shot", "gx"), "gy", None)
    return jax.shard_map(
        shards,
        mesh=mesh,
        in_specs=(block, block, block, P(), P("shot"), P("shot"), P("shot")),
        out_specs=(block, block, block),
        check_vma=False,
    )
```

```python
import functools

import jax
import jax.numpy as jnp
import ml_dtypes
import numpy as np
from jax import lax
from jax.experimental import pallas as pl
from jax.experimental.pallas import tpu as pltpu
from jax.sharding import PartitionSpec as P

STENCIL_WEIGHTS = (-205.0 / 72.0, 8.0 / 5.0, -1.0 / 5.0, 8.0 / 315.0, -1.0 / 560.0)
LIFT_ALPHA = -1.586134342
LIFT_BETA = -0.05298011854
LIFT_GAMMA = 0.8829110762
LIFT_DELTA = 0.4435068522
LIFT_SCALE = 1.149604398
DEAD_ZONE = 0.25
QUANT_STEP = 0.5
W = 4
MESH = pl.DeviceIdType.MESH
VMEM_BYTES = 32 * 1024 * 1024


def lift_matrix(size):
    field = np.eye(size + 2 * W)
    even, odd = field[0::2], field[1::2]
    odd = odd[:-1] + LIFT_ALPHA * (even[:-1] + even[1:])
    even = even[1:-1] + LIFT_BETA * (odd[:-1] + odd[1:])
    odd = odd[1:-1] + LIFT_GAMMA * (even[:-1] + even[1:])
    even = even[1:-1] + LIFT_DELTA * (odd[:-1] + odd[1:])
    out = np.zeros((size, size + 2 * W))
    out[0::2] = even / LIFT_SCALE
    out[1::2] = odd[1:] * LIFT_SCALE
    return out


def reflected(matrix, first, last):
    size = matrix.shape[0]
    out = matrix.copy()
    for step in range(1, W + 1):
        if first:
            out[:, W + step] += out[:, W - step]
            out[:, W - step] = 0.0
        if last:
            out[:, W + size - 1 - step] += out[:, W + size - 1 + step]
            out[:, W + size - 1 + step] = 0.0
    return out


def halves(matrix):
    wide = np.asarray(matrix, np.float32)
    high = wide.astype(ml_dtypes.bfloat16)
    low = (wide - high.astype(np.float32)).astype(ml_dtypes.bfloat16)
    return np.stack([high, low], axis=-3)


def halo_cells(rows_x, rows_y):
    low, x_high, y_high = range(-W, 0), range(rows_x, rows_x + W), range(rows_y, rows_y + W)
    cells = [(x, y) for x in low for y in range(rows_y)]
    cells += [(x, y) for x in x_high for y in range(rows_y)]
    cells += [(x, y) for x in range(rows_x) for y in low]
    cells += [(x, y) for x in range(rows_x) for y in y_high]
    faces = len(cells)
    for side_x in (low, x_high):
        for side_y in (low, y_high):
            cells += [(x, y) for x in side_x for y in side_y]
    return cells, faces


@functools.lru_cache(None)
def tables(rows_x, rows_y, depth):
    cells, faces = halo_cells(rows_x, rows_y)
    own = [(x, y) for x in range(rows_x) for y in range(rows_y)]
    everywhere = np.array(own + cells)
    target = np.array(own)
    gap_x = np.abs(target[:, None, 0] - everywhere[None, :, 0])
    gap_y = np.abs(target[:, None, 1] - everywhere[None, :, 1])
    weights = np.array(list(STENCIL_WEIGHTS) + [0.0])
    star = np.where(gap_y == 0, weights[np.minimum(gap_x, W + 1)], 0.0)
    star = star + np.where(gap_x == 0, weights[np.minimum(gap_y, W + 1)], 0.0)
    star = star[:, : len(own) + faces]
    spot = np.arange(depth)
    along = weights[np.minimum(np.abs(spot[:, None] - spot[None, :]), W + 1)]
    depth_lift = reflected(lift_matrix(depth), True, True)[:, W : W + depth].T
    kinds = ((False, False), (True, False), (False, True))
    lifts = []
    for kind_x in kinds:
        for kind_y in kinds:
            by_x = reflected(lift_matrix(rows_x), *kind_x)[:, everywhere[:, 0] + W]
            by_y = reflected(lift_matrix(rows_y), *kind_y)[:, everywhere[:, 1] + W]
            lifts.append(by_x[target[:, 0]] * by_y[target[:, 1]])
    lifts = np.stack(lifts)
    spare = -lifts.shape[2] % 128
    lifts = np.pad(lifts, ((0, 0), (0, 0), (0, spare)))
    depth_both = np.concatenate([halves(along), halves(depth_lift)])
    return halves(star), depth_both, halves(lifts)


def split(values):
    high = values.astype(jnp.bfloat16)
    return high, (values - high.astype(jnp.float32)).astype(jnp.bfloat16)


def product(left, right):
    dot = functools.partial(jnp.dot, preferred_element_type=jnp.float32)
    return dot(left[0], right[0]) + (dot(left[0], right[1]) + dot(left[1], right[0]))


def choose(classes, entries, bit):
    if len(entries) == 1:
        return entries[0]
    half = len(entries) // 2
    low = choose(classes, entries[:half], bit // 2)
    high = choose(classes, entries[half:], bit // 2)
    return jnp.where((classes & bit) != 0, high, low)


def kernel(
    rows_x, rows_y,
    cells_hbm, samples_hbm, wave_hbm, table_hbm,
    now_hbm, old_hbm, classes_hbm, star_hbm, along_hbm, lift_hbm,
    next_hbm, mid_hbm, code_hbm,
    cells_ref, samples_ref, wave_ref, table_ref,
    now, old, classes, star, along, lift,
    courant, mid, later, acc, packed, halo_a, halo_b, halo_c,
    local_sem, out_sem, send_sem, recv_sem,
):
    depth = now.shape[1]
    size = rows_x * rows_y
    face_x, face_y, corner = W * rows_y, W * rows_x, W * W
    faces = 2 * face_x + 2 * face_y
    at_x, at_y = lax.axis_index("gx"), lax.axis_index("gy")
    count_x, count_y = lax.axis_size("gx"), lax.axis_size("gy")
    shot = lax.axis_index("shot")
    low_x, high_x = at_x > 0, at_x < count_x - 1
    low_y, high_y = at_y > 0, at_y < count_y - 1
    kind_x = jnp.where(low_x, jnp.where(high_x, 0, 2), 1)
    kind_y = jnp.where(low_y, jnp.where(high_y, 0, 2), 1)

    pulls = [
        pltpu.make_async_copy(src, dst, local_sem.at[i])
        for i, (src, dst) in enumerate(
            [
                (now_hbm, now), (classes_hbm, classes), (old_hbm, old),
                (star_hbm, star), (along_hbm, along),
                (lift_hbm.at[kind_x * 3 + kind_y], lift),
                (cells_hbm, cells_ref), (samples_hbm, samples_ref),
                (wave_hbm, wave_ref), (table_hbm, table_ref),
            ]
        )
    ]
    for pull in pulls:
        pull.start()

    steps = ((-1, low_x, low_y), (1, high_x, high_y))
    partners = [(dx, 0, has) for dx, has, _ in steps] + [(0, dy, has) for dy, _, has in steps]
    partners += [
        (dx, dy, jnp.logical_and(has_x, has_y)) for dx, has_x, _ in steps for dy, _, has_y in steps
    ]

    def device(dx, dy):
        return {"shot": shot, "gy": at_y + dy, "gx": at_x + dx}

    barrier = pltpu.get_barrier_semaphore()
    for dx, dy, has in partners:
        @pl.when(has)
        def _(dx=dx, dy=dy):
            pl.semaphore_signal(barrier, inc=1, device_id=device(dx, dy), device_id_type=MESH)

    def pack(source, where):
        for x in range(0, rows_x, 2):
            first, second = x * rows_y, (x + 1) * rows_y
            packed[where, 0, x * W : (x + 2) * W, :] = jnp.concatenate(
                [source[first : first + W, :], source[second : second + W, :]], axis=0
            )
            packed[where, 1, x * W : (x + 2) * W, :] = jnp.concatenate(
                [source[first + rows_y - W : second, :],
                 source[second + rows_y - W : second + rows_y, :]], axis=0
            )

    slots = [(0, face_x), (face_x, face_x), (2 * face_x, face_y), (2 * face_x + face_y, face_y)]
    slots += [(faces + i * corner, corner) for i in range(4)]

    def exchange(source, halo, where, base, with_corners):
        ends = [
            source.at[pl.ds(0, face_x)],
            source.at[pl.ds(size - face_x, face_x)],
            packed.at[where, 0],
            packed.at[where, 1],
            packed.at[where, 0, pl.ds(0, corner)],
            packed.at[where, 1, pl.ds(0, corner)],
            packed.at[where, 0, pl.ds(face_y - corner, corner)],
            packed.at[where, 1, pl.ds(face_y - corner, corner)],
        ]
        opposite = [1, 0, 3, 2, 7, 6, 5, 4]
        sends, arrivals = [], []
        for i in range(8 if with_corners else 4):
            dx, dy, has = partners[i]
            for to, found in ((opposite[i], sends), (i, arrivals)):
                start, length = slots[to]
                found.append((has, pltpu.make_async_remote_copy(
                    src_ref=ends[i],
                    dst_ref=halo.at[pl.ds(start, length)],
                    send_sem=send_sem.at[base + i],
                    recv_sem=recv_sem.at[base + to],
                    device_id=device(dx, dy),
                    device_id_type=MESH,
                )))
        return sends, arrivals

    def each(copies, act):
        for has, copy in copies:
            @pl.when(has)
            def _(copy=copy):
                act(copy)

    start = lambda copy: copy.start()
    landed = lambda copy: copy.wait_recv()
    sent = lambda copy: copy.wait_send()

    first_sends, first_lands = exchange(now, halo_a, 0, 0, False)
    second_sends, second_lands = exchange(mid, halo_b, 1, 4, False)
    third_sends, third_lands = exchange(later, halo_c, 2, 8, True)

    for halo, lands in ((halo_a, first_lands), (halo_b, second_lands), (halo_c, third_lands)):
        for i, (has, _) in enumerate(lands):
            begin, length = slots[i]

            @pl.when(jnp.logical_not(has))
            def _(halo=halo, begin=begin, length=length):
                halo[begin : begin + length, :] = jnp.zeros((length, depth), jnp.float32)
    tail = faces + 4 * corner
    if halo_c.shape[0] > tail:
        halo_c[tail:, :] = jnp.zeros((halo_c.shape[0] - tail, depth), jnp.float32)

    pulls[0].wait()
    pack(now, 0)
    near_x = low_x.astype(jnp.int32) + high_x.astype(jnp.int32)
    near_y = low_y.astype(jnp.int32) + high_y.astype(jnp.int32)
    pl.semaphore_wait(barrier, near_x + near_y + near_x * near_y)
    each(first_sends[2:], start)
    each(first_sends[:2], start)

    for pull in pulls[6:]:
        pull.wait()
    wave_len = wave_ref.shape[0]
    all_y = rows_y * count_y
    shots = []
    for s in range(cells_ref.shape[0]):
        cell, sample = cells_ref[s], samples_ref[s]
        cell_x = lax.div(cell, all_y * depth) - at_x * rows_x
        cell_y = lax.rem(lax.div(cell, depth), all_y) - at_y * rows_y
        here = (cell_x >= 0) & (cell_x < rows_x) & (cell_y >= 0) & (cell_y < rows_y)
        spot = jnp.where(here, (cell_x * rows_y + cell_y) * depth + lax.rem(cell, depth), -1)
        following = jnp.where(sample + 1 >= wave_len, 0, sample + 1)
        shots.append((spot, wave_ref[sample], wave_ref[following]))
    entries = [table_ref[i] for i in range(table_ref.shape[0])]
    while len(entries) & (len(entries) - 1):
        entries.append(entries[-1])
    pulls[1].wait()
    pulls[2].wait()

    def plane(x, carry):
        rows = pl.ds(pl.multiple_of(x * rows_y, rows_y), rows_y)
        courant[rows, :] = jnp.broadcast_to(
            choose(classes[rows, :], entries, len(entries) // 2), (rows_y, depth)
        )
        place = lax.broadcasted_iota(jnp.int32, (rows_y, depth), 0) * depth
        place = place + lax.broadcasted_iota(jnp.int32, (rows_y, depth), 1)
        here = now[rows, :]
        base_a = 2.0 * here - old[rows, :]
        base_b = -here
        for spot, amp_a, amp_b in shots:
            hit = place == spot - x * (rows_y * depth)
            base_a = base_a + jnp.where(hit, amp_a, 0.0)
            base_b = base_b + jnp.where(hit, amp_b, 0.0)
        old[rows, :] = base_a
        later[rows, :] = base_b
        return carry

    lax.fori_loop(0, rows_x, plane, 0)
    pulls[3].wait()
    pulls[4].wait()

    def inner(field):
        both = split(field[...])
        own = [star[0, :, :size], star[1, :, :size]]
        acc[...] = product(own, both) + product(both, (along[0], along[1]))

    def outer(halo):
        return product([star[0, :, size:], star[1, :, size:]], split(halo[...]))

    inner(now)
    each(first_lands, landed)
    mid[...] = old[...] + courant[...] * (acc[...] + outer(halo_a))
    each(second_sends[:2], start)
    pack(mid, 1)
    each(second_sends[2:], start)
    mid_out = pltpu.make_async_copy(mid, mid_hbm, out_sem.at[0])
    mid_out.start()

    later[...] = later[...] + 2.0 * mid[...]
    inner(mid)
    each(second_lands, landed)
    later[...] = later[...] + courant[...] * (acc[...] + outer(halo_b))
    each(third_sends[:2], start)
    pack(later, 2)
    each(third_sends[2:], start)
    next_out = pltpu.make_async_copy(later, next_hbm, out_sem.at[1])
    next_out.start()

    pulls[5].wait()
    acc[...] = product([lift[0, :, :size], lift[1, :, :size]], split(later[...]))
    each(third_lands, landed)
    lifted = acc[...] + product([lift[0, :, size:], lift[1, :, size:]], split(halo_c[...]))
    lifted = product(split(lifted), (along[2], along[3]))
    shrunk = jnp.maximum(jnp.abs(lifted) - DEAD_ZONE, 0.0) / QUANT_STEP
    acc[...] = jnp.where(lifted < 0.0, -shrunk, shrunk)
    code_out = pltpu.make_async_copy(acc, code_hbm, out_sem.at[2])
    code_out.start()
    each(first_sends, sent)
    each(second_sends, sent)
    each(third_sends, sent)
    mid_out.wait()
    next_out.wait()
    code_out.wait()


def put_out(*refs):
    sources, targets, sems = refs[:3], refs[3:6], refs[6]
    copies = [pltpu.make_async_copy(sources[i], targets[i], sems.at[i]) for i in range(3)]
    for copy in copies:
        copy.start()
    for copy in copies:
        copy.wait()


def shards(pressure_now, pressure_old, classes, class_table, wavelet, source_cells, samples):
    rows_x, rows_y, depth = pressure_now.shape
    size = rows_x * rows_y
    flat = (size, depth)
    star, along, lift = tables(rows_x, rows_y, depth)
    halo_rows = star.shape[2] - size
    wide_rows = lift.shape[3] - size
    face_y = W * rows_x
    any_spec = pl.BlockSpec(memory_space=pl.ANY)
    hbm = pl.BlockSpec(memory_space=pltpu.HBM)
    f32 = jnp.float32
    out = jax.ShapeDtypeStruct(flat, f32)
    results = pl.pallas_call(
        functools.partial(kernel, rows_x, rows_y),
        out_shape=(out, out, out),
        in_specs=[hbm] * 10,
        out_specs=(any_spec,) * 3,
        scratch_shapes=[
            pltpu.SMEM(source_cells.shape, jnp.int32),
            pltpu.SMEM(samples.shape, jnp.int32),
            pltpu.SMEM(wavelet.shape, f32),
            pltpu.SMEM(class_table.shape, f32),
            pltpu.VMEM(flat, f32),
            pltpu.VMEM(flat, f32),
            pltpu.VMEM(flat, jnp.int32),
            pltpu.VMEM(star.shape, jnp.bfloat16),
            pltpu.VMEM(along.shape, jnp.bfloat16),
            pltpu.VMEM(lift.shape[1:], jnp.bfloat16),
            pltpu.VMEM(flat, f32),
            pltpu.VMEM(flat, f32),
            pltpu.VMEM(flat, f32),
            pltpu.VMEM(flat, f32),
            pltpu.VMEM((3, 2, face_y, depth), f32),
            pltpu.VMEM((halo_rows, depth), f32),
            pltpu.VMEM((halo_rows, depth), f32),
            pltpu.VMEM((wide_rows, depth), f32),
            pltpu.SemaphoreType.DMA((10,)),
            pltpu.SemaphoreType.DMA((3,)),
            pltpu.SemaphoreType.DMA((16,)),
            pltpu.SemaphoreType.DMA((16,)),
        ],
        compiler_params=pltpu.CompilerParams(
            collective_id=0, has_side_effects=True, vmem_limit_bytes=VMEM_BYTES
        ),
    )(*[
        pltpu.with_memory_space_constraint(operand, pltpu.HBM)
        for operand in (
            source_cells, samples, wavelet, class_table,
            pressure_now.reshape(flat), pressure_old.reshape(flat), classes.reshape(flat),
            jnp.asarray(star), jnp.asarray(along), jnp.asarray(lift),
        )
    ])
    results = pl.pallas_call(
        put_out,
        out_shape=(out, out, out),
        in_specs=[any_spec] * 3,
        out_specs=(hbm,) * 3,
        scratch_shapes=[pltpu.SemaphoreType.DMA((3,))],
        compiler_params=pltpu.CompilerParams(vmem_limit_bytes=VMEM_BYTES),
    )(*results)
    return tuple(result.reshape(pressure_now.shape) for result in results)


def solution(mesh):
    block = P(("shot", "gx"), "gy", None)
    return jax.shard_map(
        shards,
        mesh=mesh,
        in_specs=(block, block, block, P(), P("shot"), P("shot"), P("shot")),
        out_specs=(block, block, block),
        check_vma=False,
    )
```

```python
import functools

import jax
import jax.numpy as jnp
import ml_dtypes
import numpy as np
from jax import lax
from jax.experimental import pallas as pl
from jax.experimental.pallas import tpu as pltpu
from jax.sharding import PartitionSpec as P

STENCIL_WEIGHTS = (-205.0 / 72.0, 8.0 / 5.0, -1.0 / 5.0, 8.0 / 315.0, -1.0 / 560.0)
LIFT_ALPHA = -1.586134342
LIFT_BETA = -0.05298011854
LIFT_GAMMA = 0.8829110762
LIFT_DELTA = 0.4435068522
LIFT_SCALE = 1.149604398
DEAD_ZONE = 0.25
QUANT_STEP = 0.5
W = 4
MESH = pl.DeviceIdType.MESH
PARTS = 2
VMEM_BYTES = 32 * 1024 * 1024


def lift_matrix(size):
    field = np.eye(size + 2 * W)
    even, odd = field[0::2], field[1::2]
    odd = odd[:-1] + LIFT_ALPHA * (even[:-1] + even[1:])
    even = even[1:-1] + LIFT_BETA * (odd[:-1] + odd[1:])
    odd = odd[1:-1] + LIFT_GAMMA * (even[:-1] + even[1:])
    even = even[1:-1] + LIFT_DELTA * (odd[:-1] + odd[1:])
    out = np.zeros((size, size + 2 * W))
    out[0::2] = even / LIFT_SCALE
    out[1::2] = odd[1:] * LIFT_SCALE
    return out


def reflected(matrix, first, last):
    size = matrix.shape[0]
    out = matrix.copy()
    for step in range(1, W + 1):
        if first:
            out[:, W + step] += out[:, W - step]
            out[:, W - step] = 0.0
        if last:
            out[:, W + size - 1 - step] += out[:, W + size - 1 + step]
            out[:, W + size - 1 + step] = 0.0
    return out


def halves(matrix):
    wide = np.asarray(matrix, np.float32)
    high = wide.astype(ml_dtypes.bfloat16)
    low = (wide - high.astype(np.float32)).astype(ml_dtypes.bfloat16)
    return np.stack([high, low], axis=-3)


def halo_cells(rows_x, rows_y):
    low, x_high, y_high = range(-W, 0), range(rows_x, rows_x + W), range(rows_y, rows_y + W)
    cells = [(x, y) for x in low for y in range(rows_y)]
    cells += [(x, y) for x in x_high for y in range(rows_y)]
    cells += [(x, y) for x in range(rows_x) for y in low]
    cells += [(x, y) for x in range(rows_x) for y in y_high]
    faces = len(cells)
    for side_x in (low, x_high):
        for side_y in (low, y_high):
            cells += [(x, y) for x in side_x for y in side_y]
    return cells, faces


@functools.lru_cache(None)
def tables(rows_x, rows_y, depth):
    cells, faces = halo_cells(rows_x, rows_y)
    own = [(x, y) for x in range(rows_x) for y in range(rows_y)]
    everywhere = np.array(own + cells)
    target = np.array(own)
    gap_x = np.abs(target[:, None, 0] - everywhere[None, :, 0])
    gap_y = np.abs(target[:, None, 1] - everywhere[None, :, 1])
    weights = np.array(list(STENCIL_WEIGHTS) + [0.0])
    star = np.where(gap_y == 0, weights[np.minimum(gap_x, W + 1)], 0.0)
    star = star + np.where(gap_x == 0, weights[np.minimum(gap_y, W + 1)], 0.0)
    star = star[:, : len(own) + faces]
    spot = np.arange(depth)
    along = weights[np.minimum(np.abs(spot[:, None] - spot[None, :]), W + 1)]
    depth_lift = reflected(lift_matrix(depth), True, True)[:, W : W + depth].T
    kinds = ((False, False), (True, False), (False, True))
    lifts = []
    for kind_x in kinds:
        for kind_y in kinds:
            by_x = reflected(lift_matrix(rows_x), *kind_x)[:, everywhere[:, 0] + W]
            by_y = reflected(lift_matrix(rows_y), *kind_y)[:, everywhere[:, 1] + W]
            lifts.append(by_x[target[:, 0]] * by_y[target[:, 1]])
    lifts = np.stack(lifts)
    spare = -lifts.shape[2] % 128
    lifts = np.pad(lifts, ((0, 0), (0, 0), (0, spare)))
    depth_both = np.concatenate([halves(along), halves(depth_lift)])
    return halves(star), depth_both, halves(lifts)


def split(values):
    high = values.astype(jnp.bfloat16)
    return high, (values - high.astype(jnp.float32)).astype(jnp.bfloat16)


def product(left, right):
    dot = functools.partial(jnp.dot, preferred_element_type=jnp.float32)
    return dot(left[0], right[0]) + (dot(left[0], right[1]) + dot(left[1], right[0]))


def choose(classes, entries, bit):
    if len(entries) == 1:
        return entries[0]
    half = len(entries) // 2
    low = choose(classes, entries[:half], bit // 2)
    high = choose(classes, entries[half:], bit // 2)
    return jnp.where((classes & bit) != 0, high, low)


def kernel(
    rows_x, rows_y,
    cells_hbm, samples_hbm, wave_hbm, table_hbm,
    now_hbm, old_hbm, classes_hbm, star_hbm, along_hbm, lift_hbm,
    next_hbm, mid_hbm, code_hbm,
    cells_ref, samples_ref, wave_ref, table_ref,
    now, old, classes, star, along, lift,
    courant, mid, later, acc, packed, halo_a, halo_b, halo_c,
    local_sem, out_sem, send_sem, recv_sem,
):
    depth = now.shape[1]
    size = rows_x * rows_y
    face_x, face_y, corner = W * rows_y, W * rows_x, W * W
    faces = 2 * face_x + 2 * face_y
    width = depth // PARTS
    at_x, at_y = lax.axis_index("gx"), lax.axis_index("gy")
    count_x, count_y = lax.axis_size("gx"), lax.axis_size("gy")
    shot = lax.axis_index("shot")
    low_x, high_x = at_x > 0, at_x < count_x - 1
    low_y, high_y = at_y > 0, at_y < count_y - 1
    kind_x = jnp.where(low_x, jnp.where(high_x, 0, 2), 1)
    kind_y = jnp.where(low_y, jnp.where(high_y, 0, 2), 1)

    pulls = [
        pltpu.make_async_copy(src, dst, local_sem.at[i])
        for i, (src, dst) in enumerate(
            [
                (now_hbm, now), (classes_hbm, classes), (old_hbm, old),
                (star_hbm, star), (along_hbm, along),
                (lift_hbm.at[kind_x * 3 + kind_y], lift),
                (cells_hbm, cells_ref), (samples_hbm, samples_ref),
                (wave_hbm, wave_ref), (table_hbm, table_ref),
            ]
        )
    ]
    for pull in pulls:
        pull.start()

    steps = ((-1, low_x, low_y), (1, high_x, high_y))
    partners = [(dx, 0, has) for dx, has, _ in steps] + [(0, dy, has) for dy, _, has in steps]
    partners += [
        (dx, dy, jnp.logical_and(has_x, has_y)) for dx, has_x, _ in steps for dy, _, has_y in steps
    ]

    def device(dx, dy):
        return {"shot": shot, "gy": at_y + dy, "gx": at_x + dx}

    barrier = pltpu.get_barrier_semaphore()
    for dx, dy, has in partners:
        @pl.when(has)
        def _(dx=dx, dy=dy):
            pl.semaphore_signal(barrier, inc=1, device_id=device(dx, dy), device_id_type=MESH)

    def pack(source, where, part):
        lanes = slice(part * width, (part + 1) * width)
        for x in range(0, rows_x, 2):
            first, second = x * rows_y, (x + 1) * rows_y
            packed[where, 0, x * W : (x + 2) * W, lanes] = jnp.concatenate(
                [source[first : first + W, lanes], source[second : second + W, lanes]], axis=0
            )
            packed[where, 1, x * W : (x + 2) * W, lanes] = jnp.concatenate(
                [source[first + rows_y - W : second, lanes],
                 source[second + rows_y - W : second + rows_y, lanes]], axis=0
            )

    slots = [(0, face_x), (face_x, face_x), (2 * face_x, face_y), (2 * face_x + face_y, face_y)]
    slots += [(faces + i * corner, corner) for i in range(4)]

    def exchange(source, halo, where, base, part, with_corners):
        lanes = pl.ds(part * width, width)
        ends = [
            source.at[pl.ds(0, face_x), lanes],
            source.at[pl.ds(size - face_x, face_x), lanes],
            packed.at[where, 0, pl.ds(0, face_y), lanes],
            packed.at[where, 1, pl.ds(0, face_y), lanes],
            packed.at[where, 0, pl.ds(0, corner), lanes],
            packed.at[where, 1, pl.ds(0, corner), lanes],
            packed.at[where, 0, pl.ds(face_y - corner, corner), lanes],
            packed.at[where, 1, pl.ds(face_y - corner, corner), lanes],
        ]
        opposite = [1, 0, 3, 2, 7, 6, 5, 4]
        sends, arrivals = [], []
        for i in range(8 if with_corners else 4):
            dx, dy, has = partners[i]
            for to, found in ((opposite[i], sends), (i, arrivals)):
                start, length = slots[to]
                found.append((has, pltpu.make_async_remote_copy(
                    src_ref=ends[i],
                    dst_ref=halo.at[pl.ds(start, length), lanes],
                    send_sem=send_sem.at[part, base + i],
                    recv_sem=recv_sem.at[part, base + to],
                    device_id=device(dx, dy),
                    device_id_type=MESH,
                )))
        return sends[2:] + sends[:2], arrivals

    def each(copies, act):
        for has, copy in copies:
            @pl.when(has)
            def _(copy=copy):
                act(copy)

    start = lambda copy: copy.start()
    landed = lambda copy: copy.wait_recv()
    sent = lambda copy: copy.wait_send()

    parts = range(PARTS)
    first = [exchange(now, halo_a, 0, 0, part, False) for part in parts]
    second = [exchange(mid, halo_b, 1, 4, part, False) for part in parts]
    third = [exchange(later, halo_c, 2, 8, part, True) for part in parts]

    for halo, lands in ((halo_a, first[0][1]), (halo_b, second[0][1]), (halo_c, third[0][1])):
        for i, (has, _) in enumerate(lands):
            begin, length = slots[i]

            @pl.when(jnp.logical_not(has))
            def _(halo=halo, begin=begin, length=length):
                halo[begin : begin + length, :] = jnp.zeros((length, depth), jnp.float32)
    tail = faces + 4 * corner
    if halo_c.shape[0] > tail:
        halo_c[tail:, :] = jnp.zeros((halo_c.shape[0] - tail, depth), jnp.float32)

    pulls[0].wait()
    for part in parts:
        pack(now, 0, part)
    near_x = low_x.astype(jnp.int32) + high_x.astype(jnp.int32)
    near_y = low_y.astype(jnp.int32) + high_y.astype(jnp.int32)
    pl.semaphore_wait(barrier, near_x + near_y + near_x * near_y)
    for part in parts:
        each(first[part][0], start)

    for pull in pulls[6:]:
        pull.wait()
    wave_len = wave_ref.shape[0]
    all_y = rows_y * count_y
    shots = []
    for s in range(cells_ref.shape[0]):
        cell, sample = cells_ref[s], samples_ref[s]
        cell_x = lax.div(cell, all_y * depth) - at_x * rows_x
        cell_y = lax.rem(lax.div(cell, depth), all_y) - at_y * rows_y
        here = (cell_x >= 0) & (cell_x < rows_x) & (cell_y >= 0) & (cell_y < rows_y)
        spot = jnp.where(here, (cell_x * rows_y + cell_y) * depth + lax.rem(cell, depth), -1)
        following = jnp.where(sample + 1 >= wave_len, 0, sample + 1)
        shots.append((spot, wave_ref[sample], wave_ref[following]))
    entries = [table_ref[i] for i in range(table_ref.shape[0])]
    while len(entries) & (len(entries) - 1):
        entries.append(entries[-1])
    pulls[1].wait()
    pulls[2].wait()

    def plane(x, carry):
        rows = pl.ds(pl.multiple_of(x * rows_y, rows_y), rows_y)
        courant[rows, :] = jnp.broadcast_to(
            choose(classes[rows, :], entries, len(entries) // 2), (rows_y, depth)
        )
        place = lax.broadcasted_iota(jnp.int32, (rows_y, depth), 0) * depth
        place = place + lax.broadcasted_iota(jnp.int32, (rows_y, depth), 1)
        here = now[rows, :]
        base_a = 2.0 * here - old[rows, :]
        base_b = -here
        for spot, amp_a, amp_b in shots:
            hit = place == spot - x * (rows_y * depth)
            base_a = base_a + jnp.where(hit, amp_a, 0.0)
            base_b = base_b + jnp.where(hit, amp_b, 0.0)
        old[rows, :] = base_a
        later[rows, :] = base_b
        return carry

    lax.fori_loop(0, rows_x, plane, 0)
    pulls[3].wait()
    pulls[4].wait()

    def inner(field):
        both = split(field[...])
        own = [star[0, :, :size], star[1, :, :size]]
        acc[...] = product(own, both) + product(both, (along[0], along[1]))

    def outer(halo, lanes):
        return product([star[0, :, size:], star[1, :, size:]], split(halo[:, lanes]))

    cuts = [slice(part * width, (part + 1) * width) for part in parts]
    inner(now)
    for part, lanes in enumerate(cuts):
        each(first[part][1], landed)
        mid[:, lanes] = old[:, lanes] + courant[:, lanes] * (acc[:, lanes] + outer(halo_a, lanes))
        pack(mid, 1, part)
        each(second[part][0], start)
    mid_out = pltpu.make_async_copy(mid, mid_hbm, out_sem.at[0])
    mid_out.start()

    later[...] = later[...] + 2.0 * mid[...]
    inner(mid)
    for part, lanes in enumerate(cuts):
        each(second[part][1], landed)
        later[:, lanes] = later[:, lanes] + courant[:, lanes] * (
            acc[:, lanes] + outer(halo_b, lanes)
        )
        pack(later, 2, part)
        each(third[part][0], start)
    next_out = pltpu.make_async_copy(later, next_hbm, out_sem.at[1])
    next_out.start()

    pulls[5].wait()
    acc[...] = product([lift[0, :, :size], lift[1, :, :size]], split(later[...]))
    lifted = None
    for part, lanes in enumerate(cuts):
        each(third[part][1], landed)
        beside = [lift[0, :, size:], lift[1, :, size:]]
        flat = acc[:, lanes] + product(beside, split(halo_c[:, lanes]))
        term = product(split(flat), (along[2, lanes, :], along[3, lanes, :]))
        lifted = term if lifted is None else lifted + term
    shrunk = jnp.maximum(jnp.abs(lifted) - DEAD_ZONE, 0.0) / QUANT_STEP
    acc[...] = jnp.where(lifted < 0.0, -shrunk, shrunk)
    code_out = pltpu.make_async_copy(acc, code_hbm, out_sem.at[2])
    code_out.start()
    for sends, _ in first + second + third:
        each(sends, sent)
    mid_out.wait()
    next_out.wait()
    code_out.wait()


def put_out(*refs):
    sources, targets, sems = refs[:3], refs[3:6], refs[6]
    copies = [pltpu.make_async_copy(sources[i], targets[i], sems.at[i]) for i in range(3)]
    for copy in copies:
        copy.start()
    for copy in copies:
        copy.wait()


def shards(pressure_now, pressure_old, classes, class_table, wavelet, source_cells, samples):
    rows_x, rows_y, depth = pressure_now.shape
    size = rows_x * rows_y
    flat = (size, depth)
    star, along, lift = tables(rows_x, rows_y, depth)
    halo_rows = star.shape[2] - size
    wide_rows = lift.shape[3] - size
    face_y = W * rows_x
    any_spec = pl.BlockSpec(memory_space=pl.ANY)
    hbm = pl.BlockSpec(memory_space=pltpu.HBM)
    f32 = jnp.float32
    out = jax.ShapeDtypeStruct(flat, f32)
    results = pl.pallas_call(
        functools.partial(kernel, rows_x, rows_y),
        out_shape=(out, out, out),
        in_specs=[hbm] * 10,
        out_specs=(any_spec,) * 3,
        scratch_shapes=[
            pltpu.SMEM(source_cells.shape, jnp.int32),
            pltpu.SMEM(samples.shape, jnp.int32),
            pltpu.SMEM(wavelet.shape, f32),
            pltpu.SMEM(class_table.shape, f32),
            pltpu.VMEM(flat, f32),
            pltpu.VMEM(flat, f32),
            pltpu.VMEM(flat, jnp.int32),
            pltpu.VMEM(star.shape, jnp.bfloat16),
            pltpu.VMEM(along.shape, jnp.bfloat16),
            pltpu.VMEM(lift.shape[1:], jnp.bfloat16),
            pltpu.VMEM(flat, f32),
            pltpu.VMEM(flat, f32),
            pltpu.VMEM(flat, f32),
            pltpu.VMEM(flat, f32),
            pltpu.VMEM((3, 2, face_y, depth), f32),
            pltpu.VMEM((halo_rows, depth), f32),
            pltpu.VMEM((halo_rows, depth), f32),
            pltpu.VMEM((wide_rows, depth), f32),
            pltpu.SemaphoreType.DMA((10,)),
            pltpu.SemaphoreType.DMA((3,)),
            pltpu.SemaphoreType.DMA((PARTS, 16)),
            pltpu.SemaphoreType.DMA((PARTS, 16)),
        ],
        compiler_params=pltpu.CompilerParams(
            collective_id=0, has_side_effects=True, vmem_limit_bytes=VMEM_BYTES
        ),
    )(*[
        pltpu.with_memory_space_constraint(operand, pltpu.HBM)
        for operand in (
            source_cells, samples, wavelet, class_table,
            pressure_now.reshape(flat), pressure_old.reshape(flat), classes.reshape(flat),
            jnp.asarray(star), jnp.asarray(along), jnp.asarray(lift),
        )
    ])
    results = pl.pallas_call(
        put_out,
        out_shape=(out, out, out),
        in_specs=[any_spec] * 3,
        out_specs=(hbm,) * 3,
        scratch_shapes=[pltpu.SemaphoreType.DMA((3,))],
        compiler_params=pltpu.CompilerParams(vmem_limit_bytes=VMEM_BYTES),
    )(*results)
    return tuple(result.reshape(pressure_now.shape) for result in results)


def solution(mesh):
    block = P(("shot", "gx"), "gy", None)
    return jax.shard_map(
        shards,
        mesh=mesh,
        in_specs=(block, block, block, P(), P("shot"), P("shot"), P("shot")),
        out_specs=(block, block, block),
        check_vma=False,
    )
```

```python
import functools

import jax
import jax.numpy as jnp
import ml_dtypes
import numpy as np
from jax import lax
from jax.experimental import pallas as pl
from jax.experimental.pallas import tpu as pltpu
from jax.sharding import PartitionSpec as P

STENCIL_WEIGHTS = (-205.0 / 72.0, 8.0 / 5.0, -1.0 / 5.0, 8.0 / 315.0, -1.0 / 560.0)
LIFT_ALPHA = -1.586134342
LIFT_BETA = -0.05298011854
LIFT_GAMMA = 0.8829110762
LIFT_DELTA = 0.4435068522
LIFT_SCALE = 1.149604398
DEAD_ZONE = 0.25
QUANT_STEP = 0.5
W = 4
MESH = pl.DeviceIdType.MESH
PARTS = 2
VMEM_BYTES = 32 * 1024 * 1024


def lift_matrix(size):
    field = np.eye(size + 2 * W)
    even, odd = field[0::2], field[1::2]
    odd = odd[:-1] + LIFT_ALPHA * (even[:-1] + even[1:])
    even = even[1:-1] + LIFT_BETA * (odd[:-1] + odd[1:])
    odd = odd[1:-1] + LIFT_GAMMA * (even[:-1] + even[1:])
    even = even[1:-1] + LIFT_DELTA * (odd[:-1] + odd[1:])
    out = np.zeros((size, size + 2 * W))
    out[0::2] = even / LIFT_SCALE
    out[1::2] = odd[1:] * LIFT_SCALE
    return out


def reflected(matrix, first, last):
    size = matrix.shape[0]
    out = matrix.copy()
    for step in range(1, W + 1):
        if first:
            out[:, W + step] += out[:, W - step]
            out[:, W - step] = 0.0
        if last:
            out[:, W + size - 1 - step] += out[:, W + size - 1 + step]
            out[:, W + size - 1 + step] = 0.0
    return out


def halves(matrix):
    wide = np.asarray(matrix, np.float32)
    high = wide.astype(ml_dtypes.bfloat16)
    low = (wide - high.astype(np.float32)).astype(ml_dtypes.bfloat16)
    return np.stack([high, low], axis=-3)


def edge_sums(size):
    low, high = np.zeros((2, size)), np.zeros((2, size))
    low[0, 0] = low[1, 1] = high[0, size - 1] = high[1, size - 2] = 1.0
    low[1, 2] = high[0, size - 2] = LIFT_ALPHA
    high[1, size - 3] = LIFT_BETA
    high[1, size - 4] = LIFT_BETA * LIFT_ALPHA
    high[1, size - 2] += LIFT_BETA * LIFT_ALPHA
    return low, high


def lift_by_sums(size, first, last):
    whole = lift_matrix(size)
    low, high = edge_sums(size)
    below = whole[:, :W] @ np.linalg.pinv(high[:, size - W :])
    above = whole[:, W + size :] @ np.linalg.pinv(low[:, :W])
    assert np.allclose(below @ high[:, size - W :], whole[:, :W], atol=1e-12)
    assert np.allclose(above @ low[:, :W], whole[:, W + size :], atol=1e-12)
    own = reflected(whole, first, last)[:, W : W + size]
    return own, below * (not first), above * (not last)


def sum_rows(own_x, sides_x, own_y, sides_y):
    rows = [np.einsum("ix,jy->ijxy", side, own_y) for side in sides_x]
    rows += [np.einsum("ix,jy->ijxy", own_x, side) for side in sides_y]
    for side_x in sides_x:
        for side_y in sides_y:
            corner = np.einsum("ix,jy->ijxy", side_x, side_y)
            rows.append(np.concatenate([corner, np.zeros_like(corner)]))
    return np.concatenate([row.reshape(-1, row.shape[2] * row.shape[3]) for row in rows])


def face_cells(rows_x, rows_y):
    low, x_high, y_high = range(-W, 0), range(rows_x, rows_x + W), range(rows_y, rows_y + W)
    cells = [(x, y) for x in low for y in range(rows_y)]
    cells += [(x, y) for x in x_high for y in range(rows_y)]
    cells += [(x, y) for x in range(rows_x) for y in low]
    cells += [(x, y) for x in range(rows_x) for y in y_high]
    return cells


@functools.lru_cache(None)
def tables(rows_x, rows_y, depth):
    cells = face_cells(rows_x, rows_y)
    own = [(x, y) for x in range(rows_x) for y in range(rows_y)]
    everywhere = np.array(own + cells)
    target = np.array(own)
    gap_x = np.abs(target[:, None, 0] - everywhere[None, :, 0])
    gap_y = np.abs(target[:, None, 1] - everywhere[None, :, 1])
    weights = np.array(list(STENCIL_WEIGHTS) + [0.0])
    star = np.where(gap_y == 0, weights[np.minimum(gap_x, W + 1)], 0.0)
    star = star + np.where(gap_x == 0, weights[np.minimum(gap_y, W + 1)], 0.0)
    spot = np.arange(depth)
    along = weights[np.minimum(np.abs(spot[:, None] - spot[None, :]), W + 1)]
    depth_lift = reflected(lift_matrix(depth), True, True)[:, W : W + depth].T
    kinds = ((False, False), (True, False), (False, True))
    lifts = []
    for kind_x in kinds:
        for kind_y in kinds:
            own_x, below_x, above_x = lift_by_sums(rows_x, *kind_x)
            own_y, below_y, above_y = lift_by_sums(rows_y, *kind_y)
            beside = sum_rows(own_x.T, (below_x.T, above_x.T), own_y.T, (below_y.T, above_y.T))
            lifts.append(np.concatenate([np.kron(own_x, own_y), beside.T], axis=1))
    lifts = np.stack(lifts)
    spare = -lifts.shape[2] % 128
    lifts = np.pad(lifts, ((0, 0), (0, 0), (0, spare)))
    sums = sum_rows(np.eye(rows_x), edge_sums(rows_x), np.eye(rows_y), edge_sums(rows_y))
    depth_both = np.concatenate([halves(along), halves(depth_lift)])
    return halves(star), depth_both, halves(lifts), halves(sums)


def split(values):
    high = values.astype(jnp.bfloat16)
    return high, (values - high.astype(jnp.float32)).astype(jnp.bfloat16)


def product(left, right):
    dot = functools.partial(jnp.dot, preferred_element_type=jnp.float32)
    return dot(left[0], right[0]) + (dot(left[0], right[1]) + dot(left[1], right[0]))


def choose(classes, entries, bit):
    if len(entries) == 1:
        return entries[0]
    half = len(entries) // 2
    low = choose(classes, entries[:half], bit // 2)
    high = choose(classes, entries[half:], bit // 2)
    return jnp.where((classes & bit) != 0, high, low)


def kernel(
    rows_x, rows_y,
    cells_hbm, samples_hbm, wave_hbm, table_hbm,
    now_hbm, old_hbm, classes_hbm, star_hbm, along_hbm, lift_hbm, sums_hbm,
    next_hbm, mid_hbm, code_hbm,
    cells_ref, samples_ref, wave_ref, table_ref,
    now, old, classes, star, along, lift, sums,
    courant, mid, later, acc, packed, bundle, halo_a, halo_b, halo_c,
    local_sem, out_sem, send_sem, recv_sem,
):
    depth = now.shape[1]
    size = rows_x * rows_y
    face_x, face_y = W * rows_y, W * rows_x
    slim_x, slim_y, corner = 2 * rows_y, 2 * rows_x, 8
    slim = 2 * slim_x + 2 * slim_y
    width = depth // PARTS
    at_x, at_y = lax.axis_index("gx"), lax.axis_index("gy")
    count_x, count_y = lax.axis_size("gx"), lax.axis_size("gy")
    shot = lax.axis_index("shot")
    low_x, high_x = at_x > 0, at_x < count_x - 1
    low_y, high_y = at_y > 0, at_y < count_y - 1
    kind_x = jnp.where(low_x, jnp.where(high_x, 0, 2), 1)
    kind_y = jnp.where(low_y, jnp.where(high_y, 0, 2), 1)

    pulls = [
        pltpu.make_async_copy(src, dst, local_sem.at[i])
        for i, (src, dst) in enumerate(
            [
                (now_hbm, now), (classes_hbm, classes), (old_hbm, old),
                (star_hbm, star), (along_hbm, along),
                (lift_hbm.at[kind_x * 3 + kind_y], lift), (sums_hbm, sums),
                (cells_hbm, cells_ref), (samples_hbm, samples_ref),
                (wave_hbm, wave_ref), (table_hbm, table_ref),
            ]
        )
    ]
    for pull in pulls:
        pull.start()

    steps = ((-1, low_x, low_y), (1, high_x, high_y))
    partners = [(dx, 0, has) for dx, has, _ in steps] + [(0, dy, has) for dy, _, has in steps]
    partners += [
        (dx, dy, jnp.logical_and(has_x, has_y)) for dx, has_x, _ in steps for dy, _, has_y in steps
    ]

    def device(dx, dy):
        return {"shot": shot, "gy": at_y + dy, "gx": at_x + dx}

    barrier = pltpu.get_barrier_semaphore()
    for dx, dy, has in partners:
        @pl.when(has)
        def _(dx=dx, dy=dy):
            pl.semaphore_signal(barrier, inc=1, device_id=device(dx, dy), device_id_type=MESH)

    def pack(source, where, part):
        lanes = slice(part * width, (part + 1) * width)
        for x in range(0, rows_x, 2):
            first, second = x * rows_y, (x + 1) * rows_y
            packed[where, 0, x * W : (x + 2) * W, lanes] = jnp.concatenate(
                [source[first : first + W, lanes], source[second : second + W, lanes]], axis=0
            )
            packed[where, 1, x * W : (x + 2) * W, lanes] = jnp.concatenate(
                [source[first + rows_y - W : second, lanes],
                 source[second + rows_y - W : second + rows_y, lanes]], axis=0
            )

    slots = [(0, face_x), (face_x, face_x), (2 * face_x, face_y), (2 * face_x + face_y, face_y)]
    thin = [(0, slim_x), (slim_x, slim_x), (2 * slim_x, slim_y), (2 * slim_x + slim_y, slim_y)]
    thin += [(slim + i * corner, corner) for i in range(4)]

    def layers(source, where, lanes):
        return [
            source.at[pl.ds(0, face_x), lanes],
            source.at[pl.ds(size - face_x, face_x), lanes],
            packed.at[where, 0, pl.ds(0, face_y), lanes],
            packed.at[where, 1, pl.ds(0, face_y), lanes],
        ]

    def combined(lanes):
        return [bundle.at[pl.ds(begin, length), lanes] for begin, length in thin]

    def exchange(ends, halo, places, base, part):
        lanes = pl.ds(part * width, width)
        ends = ends(lanes)
        opposite = [1, 0, 3, 2, 7, 6, 5, 4]
        sends, arrivals = [], []
        for i in range(len(ends)):
            dx, dy, has = partners[i]
            for to, found in ((opposite[i], sends), (i, arrivals)):
                start, length = places[to]
                found.append((has, pltpu.make_async_remote_copy(
                    src_ref=ends[i],
                    dst_ref=halo.at[pl.ds(start, length), lanes],
                    send_sem=send_sem.at[part, base + i],
                    recv_sem=recv_sem.at[part, base + to],
                    device_id=device(dx, dy),
                    device_id_type=MESH,
                )))
        return sends[2:] + sends[:2], arrivals

    def each(copies, act):
        for has, copy in copies:
            @pl.when(has)
            def _(copy=copy):
                act(copy)

    start = lambda copy: copy.start()
    landed = lambda copy: copy.wait_recv()
    sent = lambda copy: copy.wait_send()

    parts = range(PARTS)
    cuts = [slice(part * width, (part + 1) * width) for part in parts]
    first = [exchange(functools.partial(layers, now, 0), halo_a, slots, 0, p) for p in parts]
    second = [exchange(functools.partial(layers, mid, 1), halo_b, slots, 4, p) for p in parts]
    third = [exchange(combined, halo_c, thin, 8, p) for p in parts]

    for halo, places, lands in (
        (halo_a, slots, first[0][1]), (halo_b, slots, second[0][1]), (halo_c, thin, third[0][1])
    ):
        for i, (has, _) in enumerate(lands):
            begin, length = places[i]

            @pl.when(jnp.logical_not(has))
            def _(halo=halo, begin=begin, length=length):
                halo[begin : begin + length, :] = jnp.zeros((length, depth), jnp.float32)
    tail = slim + 4 * corner
    if halo_c.shape[0] > tail:
        halo_c[tail:, :] = jnp.zeros((halo_c.shape[0] - tail, depth), jnp.float32)

    pulls[0].wait()
    for part in parts:
        pack(now, 0, part)
    near_x = low_x.astype(jnp.int32) + high_x.astype(jnp.int32)
    near_y = low_y.astype(jnp.int32) + high_y.astype(jnp.int32)
    pl.semaphore_wait(barrier, near_x + near_y + near_x * near_y)
    for part in parts:
        each(first[part][0], start)

    for pull in pulls[7:]:
        pull.wait()
    wave_len = wave_ref.shape[0]
    all_y = rows_y * count_y
    shots = []
    for s in range(cells_ref.shape[0]):
        cell, sample = cells_ref[s], samples_ref[s]
        cell_x = lax.div(cell, all_y * depth) - at_x * rows_x
        cell_y = lax.rem(lax.div(cell, depth), all_y) - at_y * rows_y
        here = (cell_x >= 0) & (cell_x < rows_x) & (cell_y >= 0) & (cell_y < rows_y)
        spot = jnp.where(here, (cell_x * rows_y + cell_y) * depth + lax.rem(cell, depth), -1)
        following = jnp.where(sample + 1 >= wave_len, 0, sample + 1)
        shots.append((spot, wave_ref[sample], wave_ref[following]))
    entries = [table_ref[i] for i in range(table_ref.shape[0])]
    while len(entries) & (len(entries) - 1):
        entries.append(entries[-1])
    pulls[1].wait()
    pulls[2].wait()

    def plane(x, carry):
        rows = pl.ds(pl.multiple_of(x * rows_y, rows_y), rows_y)
        courant[rows, :] = jnp.broadcast_to(
            choose(classes[rows, :], entries, len(entries) // 2), (rows_y, depth)
        )
        place = lax.broadcasted_iota(jnp.int32, (rows_y, depth), 0) * depth
        place = place + lax.broadcasted_iota(jnp.int32, (rows_y, depth), 1)
        here = now[rows, :]
        base_a = 2.0 * here - old[rows, :]
        base_b = -here
        for spot, amp_a, amp_b in shots:
            hit = place == spot - x * (rows_y * depth)
            base_a = base_a + jnp.where(hit, amp_a, 0.0)
            base_b = base_b + jnp.where(hit, amp_b, 0.0)
        old[rows, :] = base_a
        later[rows, :] = base_b
        return carry

    lax.fori_loop(0, rows_x, plane, 0)
    pulls[3].wait()
    pulls[4].wait()

    def deep(both, at, lanes):
        return product([b[:, lanes] for b in both], [along[at, lanes, lanes], along[at + 1, lanes, lanes]])

    def crossing(both, at, source, target):
        return product(
            [b[:, source] for b in both], [along[at, source, target], along[at + 1, source, target]]
        )

    seams = [
        (slice(part * width - 128, part * width), slice(part * width, part * width + 128))
        for part in range(1, PARTS)
    ]

    def inner(field):
        both = split(field[...])
        for lanes in cuts:
            own = product([star[0, :, :size], star[1, :, :size]], [b[:, lanes] for b in both])
            acc[:, lanes] = own + deep(both, 0, lanes)
        for left, right in seams:
            acc[:, left] += crossing(both, 0, right, left)
            acc[:, right] += crossing(both, 0, left, right)

    def outer(halo, lanes):
        return product([star[0, :, size:], star[1, :, size:]], split(halo[:, lanes]))

    inner(now)
    for part, lanes in enumerate(cuts):
        each(first[part][1], landed)
        mid[:, lanes] = old[:, lanes] + courant[:, lanes] * (acc[:, lanes] + outer(halo_a, lanes))
        pack(mid, 1, part)
        each(second[part][0], start)
    mid_out = pltpu.make_async_copy(mid, mid_hbm, out_sem.at[0])
    mid_out.start()

    later[...] = later[...] + 2.0 * mid[...]
    inner(mid)
    pulls[5].wait()
    pulls[6].wait()
    lifted_own = []
    for part, lanes in enumerate(cuts):
        each(second[part][1], landed)
        later[:, lanes] = later[:, lanes] + courant[:, lanes] * (
            acc[:, lanes] + outer(halo_b, lanes)
        )
        both = split(later[:, lanes])
        bundle[:, lanes] = product((sums[0], sums[1]), both)
        each(third[part][0], start)
        lifted_own.append(both)
    next_out = pltpu.make_async_copy(later, next_hbm, out_sem.at[1])
    next_out.start()

    for lanes, both in zip(cuts, lifted_own):
        acc[:, lanes] = product([lift[0, :, :size], lift[1, :, :size]], both)
    pieces = []
    for part, lanes in enumerate(cuts):
        each(third[part][1], landed)
        beside = [lift[0, :, size:], lift[1, :, size:]]
        piece = split(acc[:, lanes] + product(beside, split(halo_c[:, lanes])))
        pieces.append(piece)
        courant[:, lanes] = product(piece, (along[2, lanes, lanes], along[3, lanes, lanes]))
        if part:
            left, right = seams[part - 1]
            over = (along[2, left, right], along[3, left, right])
            courant[:, right] += product([half[:, -128:] for half in pieces[part - 1]], over)
            back = (along[2, right, left], along[3, right, left])
            courant[:, left] += product([half[:, :128] for half in piece], back)
    lifted = courant[...]
    shrunk = jnp.maximum(jnp.abs(lifted) - DEAD_ZONE, 0.0) / QUANT_STEP
    acc[...] = jnp.where(lifted < 0.0, -shrunk, shrunk)
    code_out = pltpu.make_async_copy(acc, code_hbm, out_sem.at[2])
    code_out.start()
    for sends, _ in first + second + third:
        each(sends, sent)
    mid_out.wait()
    next_out.wait()
    code_out.wait()


def put_out(*refs):
    sources, targets, sems = refs[:3], refs[3:6], refs[6]
    copies = [pltpu.make_async_copy(sources[i], targets[i], sems.at[i]) for i in range(3)]
    for copy in copies:
        copy.start()
    for copy in copies:
        copy.wait()


def shards(pressure_now, pressure_old, classes, class_table, wavelet, source_cells, samples):
    rows_x, rows_y, depth = pressure_now.shape
    size = rows_x * rows_y
    flat = (size, depth)
    star, along, lift, sums = tables(rows_x, rows_y, depth)
    halo_rows = star.shape[2] - size
    wide_rows = lift.shape[3] - size
    face_y = W * rows_x
    any_spec = pl.BlockSpec(memory_space=pl.ANY)
    hbm = pl.BlockSpec(memory_space=pltpu.HBM)
    f32 = jnp.float32
    out = jax.ShapeDtypeStruct(flat, f32)
    results = pl.pallas_call(
        functools.partial(kernel, rows_x, rows_y),
        out_shape=(out, out, out),
        in_specs=[hbm] * 11,
        out_specs=(any_spec,) * 3,
        scratch_shapes=[
            pltpu.SMEM(source_cells.shape, jnp.int32),
            pltpu.SMEM(samples.shape, jnp.int32),
            pltpu.SMEM(wavelet.shape, f32),
            pltpu.SMEM(class_table.shape, f32),
            pltpu.VMEM(flat, f32),
            pltpu.VMEM(flat, f32),
            pltpu.VMEM(flat, jnp.int32),
            pltpu.VMEM(star.shape, jnp.bfloat16),
            pltpu.VMEM(along.shape, jnp.bfloat16),
            pltpu.VMEM(lift.shape[1:], jnp.bfloat16),
            pltpu.VMEM(sums.shape, jnp.bfloat16),
            pltpu.VMEM(flat, f32),
            pltpu.VMEM(flat, f32),
            pltpu.VMEM(flat, f32),
            pltpu.VMEM(flat, f32),
            pltpu.VMEM((2, 2, face_y, depth), f32),
            pltpu.VMEM((sums.shape[1], depth), f32),
            pltpu.VMEM((halo_rows, depth), f32),
            pltpu.VMEM((halo_rows, depth), f32),
            pltpu.VMEM((wide_rows, depth), f32),
            pltpu.SemaphoreType.DMA((11,)),
            pltpu.SemaphoreType.DMA((3,)),
            pltpu.SemaphoreType.DMA((PARTS, 16)),
            pltpu.SemaphoreType.DMA((PARTS, 16)),
        ],
        compiler_params=pltpu.CompilerParams(
            collective_id=0, has_side_effects=True, vmem_limit_bytes=VMEM_BYTES
        ),
    )(*[
        pltpu.with_memory_space_constraint(operand, pltpu.HBM)
        for operand in (
            source_cells, samples, wavelet, class_table,
            pressure_now.reshape(flat), pressure_old.reshape(flat), classes.reshape(flat),
            jnp.asarray(star), jnp.asarray(along), jnp.asarray(lift),
            jnp.asarray(sums),
        )
    ])
    results = pl.pallas_call(
        put_out,
        out_shape=(out, out, out),
        in_specs=[any_spec] * 3,
        out_specs=(hbm,) * 3,
        scratch_shapes=[pltpu.SemaphoreType.DMA((3,))],
        compiler_params=pltpu.CompilerParams(vmem_limit_bytes=VMEM_BYTES),
    )(*results)
    return tuple(result.reshape(pressure_now.shape) for result in results)


def solution(mesh):
    block = P(("shot", "gx"), "gy", None)
    return jax.shard_map(
        shards,
        mesh=mesh,
        in_specs=(block, block, block, P(), P("shot"), P("shot"), P("shot")),
        out_specs=(block, block, block),
        check_vma=False,
    )
```

```python
import functools

import jax
import jax.numpy as jnp
import ml_dtypes
import numpy as np
from jax import lax
from jax.experimental import pallas as pl
from jax.experimental.pallas import tpu as pltpu
from jax.sharding import PartitionSpec as P

STENCIL_WEIGHTS = (-205.0 / 72.0, 8.0 / 5.0, -1.0 / 5.0, 8.0 / 315.0, -1.0 / 560.0)
LIFT_ALPHA = -1.586134342
LIFT_BETA = -0.05298011854
LIFT_GAMMA = 0.8829110762
LIFT_DELTA = 0.4435068522
LIFT_SCALE = 1.149604398
DEAD_ZONE = 0.25
QUANT_STEP = 0.5
W = 4
MESH = pl.DeviceIdType.MESH
PARTS = 2
VMEM_BYTES = 32 * 1024 * 1024


def lift_matrix(size):
    field = np.eye(size + 2 * W)
    even, odd = field[0::2], field[1::2]
    odd = odd[:-1] + LIFT_ALPHA * (even[:-1] + even[1:])
    even = even[1:-1] + LIFT_BETA * (odd[:-1] + odd[1:])
    odd = odd[1:-1] + LIFT_GAMMA * (even[:-1] + even[1:])
    even = even[1:-1] + LIFT_DELTA * (odd[:-1] + odd[1:])
    out = np.zeros((size, size + 2 * W))
    out[0::2] = even / LIFT_SCALE
    out[1::2] = odd[1:] * LIFT_SCALE
    return out


def reflected(matrix, first, last):
    size = matrix.shape[0]
    out = matrix.copy()
    for step in range(1, W + 1):
        if first:
            out[:, W + step] += out[:, W - step]
            out[:, W - step] = 0.0
        if last:
            out[:, W + size - 1 - step] += out[:, W + size - 1 + step]
            out[:, W + size - 1 + step] = 0.0
    return out


def halves(matrix):
    wide = np.asarray(matrix, np.float32)
    high = wide.astype(ml_dtypes.bfloat16)
    low = (wide - high.astype(np.float32)).astype(ml_dtypes.bfloat16)
    return np.stack([high, low], axis=-3)


def edge_sums(size):
    low, high = np.zeros((2, size)), np.zeros((2, size))
    low[0, 0] = low[1, 1] = high[0, size - 1] = high[1, size - 2] = 1.0
    low[1, 2] = high[0, size - 2] = LIFT_ALPHA
    high[1, size - 3] = LIFT_BETA
    high[1, size - 4] = LIFT_BETA * LIFT_ALPHA
    high[1, size - 2] += LIFT_BETA * LIFT_ALPHA
    return low, high


def lift_by_sums(size, first, last):
    whole = lift_matrix(size)
    low, high = edge_sums(size)
    below = whole[:, :W] @ np.linalg.pinv(high[:, size - W :])
    above = whole[:, W + size :] @ np.linalg.pinv(low[:, :W])
    assert np.allclose(below @ high[:, size - W :], whole[:, :W], atol=1e-12)
    assert np.allclose(above @ low[:, :W], whole[:, W + size :], atol=1e-12)
    own = reflected(whole, first, last)[:, W : W + size]
    return own, below * (not first), above * (not last)


def sum_rows(own_x, sides_x, own_y, sides_y):
    rows = [np.einsum("ix,jy->ijxy", side, own_y) for side in sides_x]
    rows += [np.einsum("ix,jy->ijxy", own_x, side) for side in sides_y]
    for side_x in sides_x:
        for side_y in sides_y:
            corner = np.einsum("ix,jy->ijxy", side_x, side_y)
            rows.append(np.concatenate([corner, np.zeros_like(corner)]))
    return np.concatenate([row.reshape(-1, row.shape[2] * row.shape[3]) for row in rows])


def face_cells(rows_x, rows_y):
    low, x_high, y_high = range(-W, 0), range(rows_x, rows_x + W), range(rows_y, rows_y + W)
    cells = [(x, y) for x in low for y in range(rows_y)]
    cells += [(x, y) for x in x_high for y in range(rows_y)]
    cells += [(x, y) for x in range(rows_x) for y in low]
    cells += [(x, y) for x in range(rows_x) for y in y_high]
    return cells


@functools.lru_cache(None)
def tables(rows_x, rows_y, depth):
    cells = face_cells(rows_x, rows_y)
    own = [(x, y) for x in range(rows_x) for y in range(rows_y)]
    everywhere = np.array(own + cells)
    target = np.array(own)
    gap_x = np.abs(target[:, None, 0] - everywhere[None, :, 0])
    gap_y = np.abs(target[:, None, 1] - everywhere[None, :, 1])
    weights = np.array(list(STENCIL_WEIGHTS) + [0.0])
    star = np.where(gap_y == 0, weights[np.minimum(gap_x, W + 1)], 0.0)
    star = star + np.where(gap_x == 0, weights[np.minimum(gap_y, W + 1)], 0.0)
    spot = np.arange(depth)
    along = weights[np.minimum(np.abs(spot[:, None] - spot[None, :]), W + 1)]
    depth_lift = reflected(lift_matrix(depth), True, True)[:, W : W + depth].T
    kinds = ((False, False), (True, False), (False, True))
    lifts = []
    for kind_x in kinds:
        for kind_y in kinds:
            own_x, below_x, above_x = lift_by_sums(rows_x, *kind_x)
            own_y, below_y, above_y = lift_by_sums(rows_y, *kind_y)
            beside = sum_rows(own_x.T, (below_x.T, above_x.T), own_y.T, (below_y.T, above_y.T))
            lifts.append(np.concatenate([np.kron(own_x, own_y), beside.T], axis=1))
    lifts = np.stack(lifts)
    spare = -lifts.shape[2] % 128
    lifts = np.pad(lifts, ((0, 0), (0, 0), (0, spare)))
    sums = sum_rows(np.eye(rows_x), edge_sums(rows_x), np.eye(rows_y), edge_sums(rows_y))
    depth_both = np.concatenate([halves(along), halves(depth_lift)])
    return halves(star), depth_both, halves(lifts), halves(sums)


def split(values):
    high = values.astype(jnp.bfloat16)
    return high, (values - high.astype(jnp.float32)).astype(jnp.bfloat16)


def product(left, right):
    dot = functools.partial(jnp.dot, preferred_element_type=jnp.float32)
    return dot(left[0], right[0]) + (dot(left[0], right[1]) + dot(left[1], right[0]))


def choose(classes, entries, bit):
    if len(entries) == 1:
        return entries[0]
    half = len(entries) // 2
    low = choose(classes, entries[:half], bit // 2)
    high = choose(classes, entries[half:], bit // 2)
    return jnp.where((classes & bit) != 0, high, low)


def kernel(
    rows_x, rows_y,
    cells_hbm, samples_hbm, wave_hbm, table_hbm,
    now_hbm, old_hbm, classes_hbm, star_hbm, along_hbm, lift_hbm, sums_hbm,
    next_hbm, mid_hbm, code_hbm,
    cells_ref, samples_ref, wave_ref, table_ref,
    now, old, classes, star, along, lift, sums,
    courant, mid, later, acc, packed, bundle, halo_a, halo_b, halo_c,
    local_sem, out_sem, send_sem, recv_sem,
):
    depth = now.shape[1]
    size = rows_x * rows_y
    face_x, face_y = W * rows_y, W * rows_x
    slim_x, slim_y, corner = 2 * rows_y, 2 * rows_x, 8
    slim = 2 * slim_x + 2 * slim_y
    width = depth // PARTS
    at_x, at_y = lax.axis_index("gx"), lax.axis_index("gy")
    count_x, count_y = lax.axis_size("gx"), lax.axis_size("gy")
    shot = lax.axis_index("shot")
    low_x, high_x = at_x > 0, at_x < count_x - 1
    low_y, high_y = at_y > 0, at_y < count_y - 1
    kind_x = jnp.where(low_x, jnp.where(high_x, 0, 2), 1)
    kind_y = jnp.where(low_y, jnp.where(high_y, 0, 2), 1)

    pulls = [
        pltpu.make_async_copy(src, dst, local_sem.at[i])
        for i, (src, dst) in enumerate(
            [
                (now_hbm, now), (classes_hbm, classes), (old_hbm, old),
                (star_hbm, star), (along_hbm, along),
                (lift_hbm.at[kind_x * 3 + kind_y], lift), (sums_hbm, sums),
                (cells_hbm, cells_ref), (samples_hbm, samples_ref),
                (wave_hbm, wave_ref), (table_hbm, table_ref),
            ]
        )
    ]
    pulls[0].start()
    for pull in pulls[7:]:
        pull.start()

    steps = ((-1, low_x, low_y), (1, high_x, high_y))
    partners = [(dx, 0, has) for dx, has, _ in steps] + [(0, dy, has) for dy, _, has in steps]
    partners += [
        (dx, dy, jnp.logical_and(has_x, has_y)) for dx, has_x, _ in steps for dy, _, has_y in steps
    ]

    def device(dx, dy):
        return {"shot": shot, "gy": at_y + dy, "gx": at_x + dx}

    barrier = pltpu.get_barrier_semaphore()
    for dx, dy, has in partners:
        @pl.when(has)
        def _(dx=dx, dy=dy):
            pl.semaphore_signal(barrier, inc=1, device_id=device(dx, dy), device_id_type=MESH)

    def pack(source, where, part):
        lanes = slice(part * width, (part + 1) * width)
        for x in range(0, rows_x, 2):
            first, second = x * rows_y, (x + 1) * rows_y
            packed[where, 0, x * W : (x + 2) * W, lanes] = jnp.concatenate(
                [source[first : first + W, lanes], source[second : second + W, lanes]], axis=0
            )
            packed[where, 1, x * W : (x + 2) * W, lanes] = jnp.concatenate(
                [source[first + rows_y - W : second, lanes],
                 source[second + rows_y - W : second + rows_y, lanes]], axis=0
            )

    slots = [(0, face_x), (face_x, face_x), (2 * face_x, face_y), (2 * face_x + face_y, face_y)]
    thin = [(0, slim_x), (slim_x, slim_x), (2 * slim_x, slim_y), (2 * slim_x + slim_y, slim_y)]
    thin += [(slim + i * corner, corner) for i in range(4)]

    def layers(source, where, lanes):
        return [
            source.at[pl.ds(0, face_x), lanes],
            source.at[pl.ds(size - face_x, face_x), lanes],
            packed.at[where, 0, pl.ds(0, face_y), lanes],
            packed.at[where, 1, pl.ds(0, face_y), lanes],
        ]

    def combined(lanes):
        return [bundle.at[pl.ds(begin, length), lanes] for begin, length in thin]

    def exchange(ends, halo, places, base, part):
        lanes = pl.ds(part * width, width)
        ends = ends(lanes)
        opposite = [1, 0, 3, 2, 7, 6, 5, 4]
        sends, arrivals = [], []
        for i in range(len(ends)):
            dx, dy, has = partners[i]
            for to, found in ((opposite[i], sends), (i, arrivals)):
                start, length = places[to]
                found.append((has, pltpu.make_async_remote_copy(
                    src_ref=ends[i],
                    dst_ref=halo.at[pl.ds(start, length), lanes],
                    send_sem=send_sem.at[part, base + i],
                    recv_sem=recv_sem.at[part, base + to],
                    device_id=device(dx, dy),
                    device_id_type=MESH,
                )))
        return sends[2:] + sends[:2], arrivals

    def each(copies, act):
        for has, copy in copies:
            @pl.when(has)
            def _(copy=copy):
                act(copy)

    start = lambda copy: copy.start()
    landed = lambda copy: copy.wait_recv()
    sent = lambda copy: copy.wait_send()

    parts = range(PARTS)
    cuts = [slice(part * width, (part + 1) * width) for part in parts]
    first = [exchange(functools.partial(layers, now, 0), halo_a, slots, 0, p) for p in parts]
    second = [exchange(functools.partial(layers, mid, 1), halo_b, slots, 4, p) for p in parts]
    third = [exchange(combined, halo_c, thin, 8, p) for p in parts]

    for halo, places, lands in (
        (halo_a, slots, first[0][1]), (halo_b, slots, second[0][1]), (halo_c, thin, third[0][1])
    ):
        for i, (has, _) in enumerate(lands):
            begin, length = places[i]

            @pl.when(jnp.logical_not(has))
            def _(halo=halo, begin=begin, length=length):
                halo[begin : begin + length, :] = jnp.zeros((length, depth), jnp.float32)
    tail = slim + 4 * corner
    if halo_c.shape[0] > tail:
        halo_c[tail:, :] = jnp.zeros((halo_c.shape[0] - tail, depth), jnp.float32)

    pulls[0].wait()
    for pull in pulls[1:5]:
        pull.start()
    for part in parts:
        pack(now, 0, part)
    near_x = low_x.astype(jnp.int32) + high_x.astype(jnp.int32)
    near_y = low_y.astype(jnp.int32) + high_y.astype(jnp.int32)
    pl.semaphore_wait(barrier, near_x + near_y + near_x * near_y)
    for part in parts:
        each(first[part][0], start)
    for pull in pulls[5:7]:
        pull.start()

    for pull in pulls[7:]:
        pull.wait()
    wave_len = wave_ref.shape[0]
    all_y = rows_y * count_y
    shots = []
    for s in range(cells_ref.shape[0]):
        cell, sample = cells_ref[s], samples_ref[s]
        cell_x = lax.div(cell, all_y * depth) - at_x * rows_x
        cell_y = lax.rem(lax.div(cell, depth), all_y) - at_y * rows_y
        here = (cell_x >= 0) & (cell_x < rows_x) & (cell_y >= 0) & (cell_y < rows_y)
        spot = jnp.where(here, (cell_x * rows_y + cell_y) * depth + lax.rem(cell, depth), -1)
        following = jnp.where(sample + 1 >= wave_len, 0, sample + 1)
        shots.append((spot, wave_ref[sample], wave_ref[following]))
    entries = [table_ref[i] for i in range(table_ref.shape[0])]
    while len(entries) & (len(entries) - 1):
        entries.append(entries[-1])
    pulls[1].wait()
    pulls[2].wait()

    place = lax.broadcasted_iota(jnp.int32, (rows_y, depth), 0) * depth
    place = place + lax.broadcasted_iota(jnp.int32, (rows_y, depth), 1)

    def with_sources(base, x, step):
        for shot_at in shots:
            hit = place == shot_at[0] - x * (rows_y * depth)
            base = base + jnp.where(hit, shot_at[1 + step], 0.0)
        return base

    def first_plane(x, carry):
        rows = pl.ds(pl.multiple_of(x * rows_y, rows_y), rows_y)
        courant[rows, :] = jnp.broadcast_to(
            choose(classes[rows, :], entries, len(entries) // 2), (rows_y, depth)
        )
        old[rows, :] = with_sources(2.0 * now[rows, :] - old[rows, :], x, 0)
        return carry

    def second_plane(x, carry):
        rows = pl.ds(pl.multiple_of(x * rows_y, rows_y), rows_y)
        later[rows, :] = with_sources(2.0 * mid[rows, :] - now[rows, :], x, 1)
        return carry

    lax.fori_loop(0, rows_x, first_plane, 0)
    pulls[3].wait()
    pulls[4].wait()

    def deep(both, at, lanes):
        return product([b[:, lanes] for b in both], [along[at, lanes, lanes], along[at + 1, lanes, lanes]])

    def crossing(both, at, source, target):
        return product(
            [b[:, source] for b in both], [along[at, source, target], along[at + 1, source, target]]
        )

    seams = [
        (slice(part * width - 128, part * width), slice(part * width, part * width + 128))
        for part in range(1, PARTS)
    ]

    def inner(field):
        both = split(field[...])
        for lanes in cuts:
            own = product([star[0, :, :size], star[1, :, :size]], [b[:, lanes] for b in both])
            acc[:, lanes] = own + deep(both, 0, lanes)
        for left, right in seams:
            acc[:, left] += crossing(both, 0, right, left)
            acc[:, right] += crossing(both, 0, left, right)

    def outer(halo, lanes):
        return product([star[0, :, size:], star[1, :, size:]], split(halo[:, lanes]))

    inner(now)
    for part, lanes in enumerate(cuts):
        each(first[part][1], landed)
        mid[:, lanes] = old[:, lanes] + courant[:, lanes] * (acc[:, lanes] + outer(halo_a, lanes))
        pack(mid, 1, part)
        each(second[part][0], start)
    mid_out = pltpu.make_async_copy(mid, mid_hbm, out_sem.at[0])
    mid_out.start()

    lax.fori_loop(0, rows_x, second_plane, 0)
    inner(mid)
    pulls[5].wait()
    pulls[6].wait()
    lifted_own = []
    for part, lanes in enumerate(cuts):
        each(second[part][1], landed)
        later[:, lanes] = later[:, lanes] + courant[:, lanes] * (
            acc[:, lanes] + outer(halo_b, lanes)
        )
        both = split(later[:, lanes])
        bundle[:, lanes] = product((sums[0], sums[1]), both)
        each(third[part][0], start)
        lifted_own.append(both)
    next_out = pltpu.make_async_copy(later, next_hbm, out_sem.at[1])
    next_out.start()

    for lanes, both in zip(cuts, lifted_own):
        acc[:, lanes] = product([lift[0, :, :size], lift[1, :, :size]], both)
    pieces = []
    for part, lanes in enumerate(cuts):
        each(third[part][1], landed)
        beside = [lift[0, :, size:], lift[1, :, size:]]
        piece = split(acc[:, lanes] + product(beside, split(halo_c[:, lanes])))
        pieces.append(piece)
        courant[:, lanes] = product(piece, (along[2, lanes, lanes], along[3, lanes, lanes]))
        if part:
            left, right = seams[part - 1]
            over = (along[2, left, right], along[3, left, right])
            courant[:, right] += product([half[:, -128:] for half in pieces[part - 1]], over)
            back = (along[2, right, left], along[3, right, left])
            courant[:, left] += product([half[:, :128] for half in piece], back)
    lifted = courant[...]
    shrunk = jnp.maximum(jnp.abs(lifted) - DEAD_ZONE, 0.0) / QUANT_STEP
    acc[...] = jnp.where(lifted < 0.0, -shrunk, shrunk)
    code_out = pltpu.make_async_copy(acc, code_hbm, out_sem.at[2])
    code_out.start()
    for sends, _ in first + second + third:
        each(sends, sent)
    mid_out.wait()
    next_out.wait()
    code_out.wait()


def put_out(*refs):
    sources, targets, sems = refs[:3], refs[3:6], refs[6]
    copies = [pltpu.make_async_copy(sources[i], targets[i], sems.at[i]) for i in range(3)]
    for copy in copies:
        copy.start()
    for copy in copies:
        copy.wait()


def shards(pressure_now, pressure_old, classes, class_table, wavelet, source_cells, samples):
    rows_x, rows_y, depth = pressure_now.shape
    size = rows_x * rows_y
    flat = (size, depth)
    star, along, lift, sums = tables(rows_x, rows_y, depth)
    halo_rows = star.shape[2] - size
    wide_rows = lift.shape[3] - size
    face_y = W * rows_x
    any_spec = pl.BlockSpec(memory_space=pl.ANY)
    hbm = pl.BlockSpec(memory_space=pltpu.HBM)
    f32 = jnp.float32
    out = jax.ShapeDtypeStruct(flat, f32)
    results = pl.pallas_call(
        functools.partial(kernel, rows_x, rows_y),
        out_shape=(out, out, out),
        in_specs=[hbm] * 11,
        out_specs=(any_spec,) * 3,
        scratch_shapes=[
            pltpu.SMEM(source_cells.shape, jnp.int32),
            pltpu.SMEM(samples.shape, jnp.int32),
            pltpu.SMEM(wavelet.shape, f32),
            pltpu.SMEM(class_table.shape, f32),
            pltpu.VMEM(flat, f32),
            pltpu.VMEM(flat, f32),
            pltpu.VMEM(flat, jnp.int32),
            pltpu.VMEM(star.shape, jnp.bfloat16),
            pltpu.VMEM(along.shape, jnp.bfloat16),
            pltpu.VMEM(lift.shape[1:], jnp.bfloat16),
            pltpu.VMEM(sums.shape, jnp.bfloat16),
            pltpu.VMEM(flat, f32),
            pltpu.VMEM(flat, f32),
            pltpu.VMEM(flat, f32),
            pltpu.VMEM(flat, f32),
            pltpu.VMEM((2, 2, face_y, depth), f32),
            pltpu.VMEM((sums.shape[1], depth), f32),
            pltpu.VMEM((halo_rows, depth), f32),
            pltpu.VMEM((halo_rows, depth), f32),
            pltpu.VMEM((wide_rows, depth), f32),
            pltpu.SemaphoreType.DMA((11,)),
            pltpu.SemaphoreType.DMA((3,)),
            pltpu.SemaphoreType.DMA((PARTS, 16)),
            pltpu.SemaphoreType.DMA((PARTS, 16)),
        ],
        compiler_params=pltpu.CompilerParams(
            collective_id=0, has_side_effects=True, vmem_limit_bytes=VMEM_BYTES
        ),
    )(*[
        pltpu.with_memory_space_constraint(operand, pltpu.HBM)
        for operand in (
            source_cells, samples, wavelet, class_table,
            pressure_now.reshape(flat), pressure_old.reshape(flat), classes.reshape(flat),
            jnp.asarray(star), jnp.asarray(along), jnp.asarray(lift),
            jnp.asarray(sums),
        )
    ])
    results = pl.pallas_call(
        put_out,
        out_shape=(out, out, out),
        in_specs=[any_spec] * 3,
        out_specs=(hbm,) * 3,
        scratch_shapes=[pltpu.SemaphoreType.DMA((3,))],
        compiler_params=pltpu.CompilerParams(vmem_limit_bytes=VMEM_BYTES),
    )(*results)
    return tuple(result.reshape(pressure_now.shape) for result in results)


def solution(mesh):
    block = P(("shot", "gx"), "gy", None)
    return jax.shard_map(
        shards,
        mesh=mesh,
        in_specs=(block, block, block, P(), P("shot"), P("shot"), P("shot")),
        out_specs=(block, block, block),
        check_vma=False,
    )
```

```python
import functools

import jax
import jax.numpy as jnp
import ml_dtypes
import numpy as np
from jax import lax
from jax.experimental import pallas as pl
from jax.experimental.pallas import tpu as pltpu
from jax.sharding import PartitionSpec as P

STENCIL_WEIGHTS = (-205.0 / 72.0, 8.0 / 5.0, -1.0 / 5.0, 8.0 / 315.0, -1.0 / 560.0)
LIFT_ALPHA = -1.586134342
LIFT_BETA = -0.05298011854
LIFT_GAMMA = 0.8829110762
LIFT_DELTA = 0.4435068522
LIFT_SCALE = 1.149604398
DEAD_ZONE = 0.25
QUANT_STEP = 0.5
W = 4
MESH = pl.DeviceIdType.MESH
PARTS = 4
VMEM_BYTES = 32 * 1024 * 1024


def lift_matrix(size):
    field = np.eye(size + 2 * W)
    even, odd = field[0::2], field[1::2]
    odd = odd[:-1] + LIFT_ALPHA * (even[:-1] + even[1:])
    even = even[1:-1] + LIFT_BETA * (odd[:-1] + odd[1:])
    odd = odd[1:-1] + LIFT_GAMMA * (even[:-1] + even[1:])
    even = even[1:-1] + LIFT_DELTA * (odd[:-1] + odd[1:])
    out = np.zeros((size, size + 2 * W))
    out[0::2] = even / LIFT_SCALE
    out[1::2] = odd[1:] * LIFT_SCALE
    return out


def reflected(matrix, first, last):
    size = matrix.shape[0]
    out = matrix.copy()
    for step in range(1, W + 1):
        if first:
            out[:, W + step] += out[:, W - step]
            out[:, W - step] = 0.0
        if last:
            out[:, W + size - 1 - step] += out[:, W + size - 1 + step]
            out[:, W + size - 1 + step] = 0.0
    return out


def halves(matrix):
    wide = np.asarray(matrix, np.float32)
    high = wide.astype(ml_dtypes.bfloat16)
    low = (wide - high.astype(np.float32)).astype(ml_dtypes.bfloat16)
    return np.stack([high, low], axis=-3)


def edge_sums(size):
    low, high = np.zeros((2, size)), np.zeros((2, size))
    low[0, 0] = low[1, 1] = high[0, size - 1] = high[1, size - 2] = 1.0
    low[1, 2] = high[0, size - 2] = LIFT_ALPHA
    high[1, size - 3] = LIFT_BETA
    high[1, size - 4] = LIFT_BETA * LIFT_ALPHA
    high[1, size - 2] += LIFT_BETA * LIFT_ALPHA
    return low, high


def lift_by_sums(size, first, last):
    whole = lift_matrix(size)
    low, high = edge_sums(size)
    below = whole[:, :W] @ np.linalg.pinv(high[:, size - W :])
    above = whole[:, W + size :] @ np.linalg.pinv(low[:, :W])
    assert np.allclose(below @ high[:, size - W :], whole[:, :W], atol=1e-12)
    assert np.allclose(above @ low[:, :W], whole[:, W + size :], atol=1e-12)
    own = reflected(whole, first, last)[:, W : W + size]
    return own, below * (not first), above * (not last)


def sum_rows(own_x, sides_x, own_y, sides_y):
    rows = [np.einsum("ix,jy->ijxy", side, own_y) for side in sides_x]
    rows += [np.einsum("ix,jy->ijxy", own_x, side) for side in sides_y]
    for side_x in sides_x:
        for side_y in sides_y:
            corner = np.einsum("ix,jy->ijxy", side_x, side_y)
            rows.append(np.concatenate([corner, np.zeros_like(corner)]))
    return np.concatenate([row.reshape(-1, row.shape[2] * row.shape[3]) for row in rows])


def face_cells(rows_x, rows_y):
    low, x_high, y_high = range(-W, 0), range(rows_x, rows_x + W), range(rows_y, rows_y + W)
    cells = [(x, y) for x in low for y in range(rows_y)]
    cells += [(x, y) for x in x_high for y in range(rows_y)]
    cells += [(x, y) for x in range(rows_x) for y in low]
    cells += [(x, y) for x in range(rows_x) for y in y_high]
    return cells


@functools.lru_cache(None)
def tables(rows_x, rows_y, depth):
    cells = face_cells(rows_x, rows_y)
    own = [(x, y) for x in range(rows_x) for y in range(rows_y)]
    everywhere = np.array(own + cells)
    target = np.array(own)
    gap_x = np.abs(target[:, None, 0] - everywhere[None, :, 0])
    gap_y = np.abs(target[:, None, 1] - everywhere[None, :, 1])
    weights = np.array(list(STENCIL_WEIGHTS) + [0.0])
    star = np.where(gap_y == 0, weights[np.minimum(gap_x, W + 1)], 0.0)
    star = star + np.where(gap_x == 0, weights[np.minimum(gap_y, W + 1)], 0.0)
    spot = np.arange(depth)
    along = weights[np.minimum(np.abs(spot[:, None] - spot[None, :]), W + 1)]
    depth_lift = reflected(lift_matrix(depth), True, True)[:, W : W + depth].T
    kinds = ((False, False), (True, False), (False, True))
    lifts = []
    for kind_x in kinds:
        for kind_y in kinds:
            own_x, below_x, above_x = lift_by_sums(rows_x, *kind_x)
            own_y, below_y, above_y = lift_by_sums(rows_y, *kind_y)
            beside = sum_rows(own_x.T, (below_x.T, above_x.T), own_y.T, (below_y.T, above_y.T))
            lifts.append(np.concatenate([np.kron(own_x, own_y), beside.T], axis=1))
    lifts = np.stack(lifts)
    spare = -lifts.shape[2] % 128
    lifts = np.pad(lifts, ((0, 0), (0, 0), (0, spare)))
    sums = sum_rows(np.eye(rows_x), edge_sums(rows_x), np.eye(rows_y), edge_sums(rows_y))
    depth_both = np.concatenate([halves(along), halves(depth_lift)])
    return halves(star), depth_both, halves(lifts), halves(sums)


def split(values):
    high = values.astype(jnp.bfloat16)
    return high, (values - high.astype(jnp.float32)).astype(jnp.bfloat16)


def product(left, right):
    dot = functools.partial(jnp.dot, preferred_element_type=jnp.float32)
    return dot(left[0], right[0]) + (dot(left[0], right[1]) + dot(left[1], right[0]))


def choose(classes, entries, bit):
    if len(entries) == 1:
        return entries[0]
    half = len(entries) // 2
    low = choose(classes, entries[:half], bit // 2)
    high = choose(classes, entries[half:], bit // 2)
    return jnp.where((classes & bit) != 0, high, low)


def kernel(
    rows_x, rows_y,
    cells_hbm, samples_hbm, wave_hbm, table_hbm,
    now_hbm, old_hbm, classes_hbm, star_hbm, along_hbm, lift_hbm, sums_hbm,
    next_hbm, mid_hbm, code_hbm,
    cells_ref, samples_ref, wave_ref, table_ref,
    now, old, classes, star, along, lift, sums,
    courant, mid, later, acc, packed, bundle, halo_a, halo_b, halo_c,
    local_sem, out_sem, send_sem, recv_sem,
):
    depth = now.shape[1]
    size = rows_x * rows_y
    face_x, face_y = W * rows_y, W * rows_x
    slim_x, slim_y, corner = 2 * rows_y, 2 * rows_x, 8
    slim = 2 * slim_x + 2 * slim_y
    width = depth // PARTS
    at_x, at_y = lax.axis_index("gx"), lax.axis_index("gy")
    count_x, count_y = lax.axis_size("gx"), lax.axis_size("gy")
    shot = lax.axis_index("shot")
    low_x, high_x = at_x > 0, at_x < count_x - 1
    low_y, high_y = at_y > 0, at_y < count_y - 1
    kind_x = jnp.where(low_x, jnp.where(high_x, 0, 2), 1)
    kind_y = jnp.where(low_y, jnp.where(high_y, 0, 2), 1)

    pulls = [
        pltpu.make_async_copy(src, dst, local_sem.at[i])
        for i, (src, dst) in enumerate(
            [
                (now_hbm, now), (classes_hbm, classes), (old_hbm, old),
                (star_hbm, star), (along_hbm, along),
                (lift_hbm.at[kind_x * 3 + kind_y], lift), (sums_hbm, sums),
                (cells_hbm, cells_ref), (samples_hbm, samples_ref),
                (wave_hbm, wave_ref), (table_hbm, table_ref),
            ]
        )
    ]
    pulls[0].start()
    for pull in pulls[7:]:
        pull.start()

    steps = ((-1, low_x, low_y), (1, high_x, high_y))
    partners = [(dx, 0, has) for dx, has, _ in steps] + [(0, dy, has) for dy, _, has in steps]
    partners += [
        (dx, dy, jnp.logical_and(has_x, has_y)) for dx, has_x, _ in steps for dy, _, has_y in steps
    ]

    def device(dx, dy):
        return {"shot": shot, "gy": at_y + dy, "gx": at_x + dx}

    barrier = pltpu.get_barrier_semaphore()
    for dx, dy, has in partners:
        @pl.when(has)
        def _(dx=dx, dy=dy):
            pl.semaphore_signal(barrier, inc=1, device_id=device(dx, dy), device_id_type=MESH)

    def pack(source, where, part):
        lanes = slice(part * width, (part + 1) * width)
        for x in range(0, rows_x, 2):
            first, second = x * rows_y, (x + 1) * rows_y
            packed[where, 0, x * W : (x + 2) * W, lanes] = jnp.concatenate(
                [source[first : first + W, lanes], source[second : second + W, lanes]], axis=0
            )
            packed[where, 1, x * W : (x + 2) * W, lanes] = jnp.concatenate(
                [source[first + rows_y - W : second, lanes],
                 source[second + rows_y - W : second + rows_y, lanes]], axis=0
            )

    slots = [(0, face_x), (face_x, face_x), (2 * face_x, face_y), (2 * face_x + face_y, face_y)]
    thin = [(0, slim_x), (slim_x, slim_x), (2 * slim_x, slim_y), (2 * slim_x + slim_y, slim_y)]
    thin += [(slim + i * corner, corner) for i in range(4)]

    def layers(source, where, lanes):
        return [
            source.at[pl.ds(0, face_x), lanes],
            source.at[pl.ds(size - face_x, face_x), lanes],
            packed.at[where, 0, pl.ds(0, face_y), lanes],
            packed.at[where, 1, pl.ds(0, face_y), lanes],
        ]

    def combined(lanes):
        return [bundle.at[pl.ds(begin, length), lanes] for begin, length in thin]

    def exchange(ends, halo, places, base, part):
        lanes = pl.ds(part * width, width)
        ends = ends(lanes)
        opposite = [1, 0, 3, 2, 7, 6, 5, 4]
        sends, arrivals = [], []
        for i in range(len(ends)):
            dx, dy, has = partners[i]
            for to, found in ((opposite[i], sends), (i, arrivals)):
                start, length = places[to]
                found.append((has, pltpu.make_async_remote_copy(
                    src_ref=ends[i],
                    dst_ref=halo.at[pl.ds(start, length), lanes],
                    send_sem=send_sem.at[part, base + i],
                    recv_sem=recv_sem.at[part, base + to],
                    device_id=device(dx, dy),
                    device_id_type=MESH,
                )))
        return sends[2:] + sends[:2], arrivals

    def each(copies, act):
        for has, copy in copies:
            @pl.when(has)
            def _(copy=copy):
                act(copy)

    start = lambda copy: copy.start()
    landed = lambda copy: copy.wait_recv()
    sent = lambda copy: copy.wait_send()

    parts = range(PARTS)
    cuts = [slice(part * width, (part + 1) * width) for part in parts]
    first = [exchange(functools.partial(layers, now, 0), halo_a, slots, 0, p) for p in parts]
    second = [exchange(functools.partial(layers, mid, 1), halo_b, slots, 4, p) for p in parts]
    third = [exchange(combined, halo_c, thin, 8, p) for p in parts]

    for halo, places, lands in (
        (halo_a, slots, first[0][1]), (halo_b, slots, second[0][1]), (halo_c, thin, third[0][1])
    ):
        for i, (has, _) in enumerate(lands):
            begin, length = places[i]

            @pl.when(jnp.logical_not(has))
            def _(halo=halo, begin=begin, length=length):
                halo[begin : begin + length, :] = jnp.zeros((length, depth), jnp.float32)
    tail = slim + 4 * corner
    if halo_c.shape[0] > tail:
        halo_c[tail:, :] = jnp.zeros((halo_c.shape[0] - tail, depth), jnp.float32)

    pulls[0].wait()
    for pull in pulls[1:5]:
        pull.start()
    for part in parts:
        pack(now, 0, part)
    near_x = low_x.astype(jnp.int32) + high_x.astype(jnp.int32)
    near_y = low_y.astype(jnp.int32) + high_y.astype(jnp.int32)
    pl.semaphore_wait(barrier, near_x + near_y + near_x * near_y)
    for part in parts:
        each(first[part][0], start)
    for pull in pulls[5:7]:
        pull.start()

    for pull in pulls[7:]:
        pull.wait()
    wave_len = wave_ref.shape[0]
    all_y = rows_y * count_y
    shots = []
    for s in range(cells_ref.shape[0]):
        cell, sample = cells_ref[s], samples_ref[s]
        cell_x = lax.div(cell, all_y * depth) - at_x * rows_x
        cell_y = lax.rem(lax.div(cell, depth), all_y) - at_y * rows_y
        here = (cell_x >= 0) & (cell_x < rows_x) & (cell_y >= 0) & (cell_y < rows_y)
        spot = jnp.where(here, (cell_x * rows_y + cell_y) * depth + lax.rem(cell, depth), -1)
        following = jnp.where(sample + 1 >= wave_len, 0, sample + 1)
        shots.append((spot, wave_ref[sample], wave_ref[following]))
    entries = [table_ref[i] for i in range(table_ref.shape[0])]
    while len(entries) & (len(entries) - 1):
        entries.append(entries[-1])
    pulls[1].wait()
    pulls[2].wait()

    place = lax.broadcasted_iota(jnp.int32, (rows_y, depth), 0) * depth
    place = place + lax.broadcasted_iota(jnp.int32, (rows_y, depth), 1)

    def with_sources(base, x, step):
        for shot_at in shots:
            hit = place == shot_at[0] - x * (rows_y * depth)
            base = base + jnp.where(hit, shot_at[1 + step], 0.0)
        return base

    def first_plane(x, carry):
        rows = pl.ds(pl.multiple_of(x * rows_y, rows_y), rows_y)
        courant[rows, :] = jnp.broadcast_to(
            choose(classes[rows, :], entries, len(entries) // 2), (rows_y, depth)
        )
        old[rows, :] = with_sources(2.0 * now[rows, :] - old[rows, :], x, 0)
        return carry

    def second_plane(x, carry):
        rows = pl.ds(pl.multiple_of(x * rows_y, rows_y), rows_y)
        later[rows, :] = with_sources(2.0 * mid[rows, :] - now[rows, :], x, 1)
        return carry

    lax.fori_loop(0, rows_x, first_plane, 0)
    pulls[3].wait()
    pulls[4].wait()

    def deep(both, at, lanes):
        return product([b[:, lanes] for b in both], [along[at, lanes, lanes], along[at + 1, lanes, lanes]])

    def crossing(both, at, source, target):
        return product(
            [b[:, source] for b in both], [along[at, source, target], along[at + 1, source, target]]
        )

    seams = [
        (slice(part * width - 128, part * width), slice(part * width, part * width + 128))
        for part in range(1, PARTS)
    ]

    def inner(field):
        both = split(field[...])
        for lanes in cuts:
            own = product([star[0, :, :size], star[1, :, :size]], [b[:, lanes] for b in both])
            acc[:, lanes] = own + deep(both, 0, lanes)
        for left, right in seams:
            acc[:, left] += crossing(both, 0, right, left)
            acc[:, right] += crossing(both, 0, left, right)

    def outer(halo, lanes):
        return product([star[0, :, size:], star[1, :, size:]], split(halo[:, lanes]))

    inner(now)
    for part, lanes in enumerate(cuts):
        each(first[part][1], landed)
        mid[:, lanes] = old[:, lanes] + courant[:, lanes] * (acc[:, lanes] + outer(halo_a, lanes))
        pack(mid, 1, part)
        each(second[part][0], start)
    mid_out = pltpu.make_async_copy(mid, mid_hbm, out_sem.at[0])
    mid_out.start()

    lax.fori_loop(0, rows_x, second_plane, 0)
    inner(mid)
    pulls[5].wait()
    pulls[6].wait()
    lifted_own = []
    for part, lanes in enumerate(cuts):
        each(second[part][1], landed)
        later[:, lanes] = later[:, lanes] + courant[:, lanes] * (
            acc[:, lanes] + outer(halo_b, lanes)
        )
        both = split(later[:, lanes])
        bundle[:, lanes] = product((sums[0], sums[1]), both)
        each(third[part][0], start)
        lifted_own.append(both)
    next_out = pltpu.make_async_copy(later, next_hbm, out_sem.at[1])
    next_out.start()

    for lanes, both in zip(cuts, lifted_own):
        acc[:, lanes] = product([lift[0, :, :size], lift[1, :, :size]], both)
    pieces = []
    for part, lanes in enumerate(cuts):
        each(third[part][1], landed)
        beside = [lift[0, :, size:], lift[1, :, size:]]
        piece = split(acc[:, lanes] + product(beside, split(halo_c[:, lanes])))
        pieces.append(piece)
        courant[:, lanes] = product(piece, (along[2, lanes, lanes], along[3, lanes, lanes]))
        if part:
            left, right = seams[part - 1]
            over = (along[2, left, right], along[3, left, right])
            courant[:, right] += product([half[:, -128:] for half in pieces[part - 1]], over)
            back = (along[2, right, left], along[3, right, left])
            courant[:, left] += product([half[:, :128] for half in piece], back)
    lifted = courant[...]
    shrunk = jnp.maximum(jnp.abs(lifted) - DEAD_ZONE, 0.0) / QUANT_STEP
    acc[...] = jnp.where(lifted < 0.0, -shrunk, shrunk)
    code_out = pltpu.make_async_copy(acc, code_hbm, out_sem.at[2])
    code_out.start()
    for sends, _ in first + second + third:
        each(sends, sent)
    mid_out.wait()
    next_out.wait()
    code_out.wait()


def put_out(*refs):
    sources, targets, sems = refs[:3], refs[3:6], refs[6]
    copies = [pltpu.make_async_copy(sources[i], targets[i], sems.at[i]) for i in range(3)]
    for copy in copies:
        copy.start()
    for copy in copies:
        copy.wait()


def shards(pressure_now, pressure_old, classes, class_table, wavelet, source_cells, samples):
    rows_x, rows_y, depth = pressure_now.shape
    size = rows_x * rows_y
    flat = (size, depth)
    star, along, lift, sums = tables(rows_x, rows_y, depth)
    halo_rows = star.shape[2] - size
    wide_rows = lift.shape[3] - size
    face_y = W * rows_x
    any_spec = pl.BlockSpec(memory_space=pl.ANY)
    hbm = pl.BlockSpec(memory_space=pltpu.HBM)
    f32 = jnp.float32
    out = jax.ShapeDtypeStruct(flat, f32)
    results = pl.pallas_call(
        functools.partial(kernel, rows_x, rows_y),
        out_shape=(out, out, out),
        in_specs=[hbm] * 11,
        out_specs=(any_spec,) * 3,
        scratch_shapes=[
            pltpu.SMEM(source_cells.shape, jnp.int32),
            pltpu.SMEM(samples.shape, jnp.int32),
            pltpu.SMEM(wavelet.shape, f32),
            pltpu.SMEM(class_table.shape, f32),
            pltpu.VMEM(flat, f32),
            pltpu.VMEM(flat, f32),
            pltpu.VMEM(flat, jnp.int32),
            pltpu.VMEM(star.shape, jnp.bfloat16),
            pltpu.VMEM(along.shape, jnp.bfloat16),
            pltpu.VMEM(lift.shape[1:], jnp.bfloat16),
            pltpu.VMEM(sums.shape, jnp.bfloat16),
            pltpu.VMEM(flat, f32),
            pltpu.VMEM(flat, f32),
            pltpu.VMEM(flat, f32),
            pltpu.VMEM(flat, f32),
            pltpu.VMEM((2, 2, face_y, depth), f32),
            pltpu.VMEM((sums.shape[1], depth), f32),
            pltpu.VMEM((halo_rows, depth), f32),
            pltpu.VMEM((halo_rows, depth), f32),
            pltpu.VMEM((wide_rows, depth), f32),
            pltpu.SemaphoreType.DMA((11,)),
            pltpu.SemaphoreType.DMA((3,)),
            pltpu.SemaphoreType.DMA((PARTS, 16)),
            pltpu.SemaphoreType.DMA((PARTS, 16)),
        ],
        compiler_params=pltpu.CompilerParams(
            collective_id=0, has_side_effects=True, vmem_limit_bytes=VMEM_BYTES
        ),
    )(*[
        pltpu.with_memory_space_constraint(operand, pltpu.HBM)
        for operand in (
            source_cells, samples, wavelet, class_table,
            pressure_now.reshape(flat), pressure_old.reshape(flat), classes.reshape(flat),
            jnp.asarray(star), jnp.asarray(along), jnp.asarray(lift),
            jnp.asarray(sums),
        )
    ])
    results = pl.pallas_call(
        put_out,
        out_shape=(out, out, out),
        in_specs=[any_spec] * 3,
        out_specs=(hbm,) * 3,
        scratch_shapes=[pltpu.SemaphoreType.DMA((3,))],
        compiler_params=pltpu.CompilerParams(vmem_limit_bytes=VMEM_BYTES),
    )(*results)
    return tuple(result.reshape(pressure_now.shape) for result in results)


def solution(mesh):
    block = P(("shot", "gx"), "gy", None)
    return jax.shard_map(
        shards,
        mesh=mesh,
        in_specs=(block, block, block, P(), P("shot"), P("shot"), P("shot")),
        out_specs=(block, block, block),
        check_vma=False,
    )
```

```python
import functools

import jax
import jax.numpy as jnp
import ml_dtypes
import numpy as np
from jax import lax
from jax.experimental import pallas as pl
from jax.experimental.pallas import tpu as pltpu
from jax.sharding import PartitionSpec as P

STENCIL_WEIGHTS = (-205.0 / 72.0, 8.0 / 5.0, -1.0 / 5.0, 8.0 / 315.0, -1.0 / 560.0)
LIFT_ALPHA = -1.586134342
LIFT_BETA = -0.05298011854
LIFT_GAMMA = 0.8829110762
LIFT_DELTA = 0.4435068522
LIFT_SCALE = 1.149604398
DEAD_ZONE = 0.25
QUANT_STEP = 0.5
W = 4
MESH = pl.DeviceIdType.MESH
PARTS = 2
VMEM_BYTES = 32 * 1024 * 1024


def lift_matrix(size):
    field = np.eye(size + 2 * W)
    even, odd = field[0::2], field[1::2]
    odd = odd[:-1] + LIFT_ALPHA * (even[:-1] + even[1:])
    even = even[1:-1] + LIFT_BETA * (odd[:-1] + odd[1:])
    odd = odd[1:-1] + LIFT_GAMMA * (even[:-1] + even[1:])
    even = even[1:-1] + LIFT_DELTA * (odd[:-1] + odd[1:])
    out = np.zeros((size, size + 2 * W))
    out[0::2] = even / LIFT_SCALE
    out[1::2] = odd[1:] * LIFT_SCALE
    return out


def reflected(matrix, first, last):
    size = matrix.shape[0]
    out = matrix.copy()
    for step in range(1, W + 1):
        if first:
            out[:, W + step] += out[:, W - step]
            out[:, W - step] = 0.0
        if last:
            out[:, W + size - 1 - step] += out[:, W + size - 1 + step]
            out[:, W + size - 1 + step] = 0.0
    return out


def halves(matrix):
    wide = np.asarray(matrix, np.float32)
    high = wide.astype(ml_dtypes.bfloat16)
    low = (wide - high.astype(np.float32)).astype(ml_dtypes.bfloat16)
    return np.stack([high, low], axis=-3)


def edge_sums(size):
    low, high = np.zeros((2, size)), np.zeros((2, size))
    low[0, 0] = low[1, 1] = high[0, size - 1] = high[1, size - 2] = 1.0
    low[1, 2] = high[0, size - 2] = LIFT_ALPHA
    high[1, size - 3] = LIFT_BETA
    high[1, size - 4] = LIFT_BETA * LIFT_ALPHA
    high[1, size - 2] += LIFT_BETA * LIFT_ALPHA
    return low, high


def lift_by_sums(size, first, last):
    whole = lift_matrix(size)
    low, high = edge_sums(size)
    below = whole[:, :W] @ np.linalg.pinv(high[:, size - W :])
    above = whole[:, W + size :] @ np.linalg.pinv(low[:, :W])
    assert np.allclose(below @ high[:, size - W :], whole[:, :W], atol=1e-12)
    assert np.allclose(above @ low[:, :W], whole[:, W + size :], atol=1e-12)
    own = reflected(whole, first, last)[:, W : W + size]
    return own, below * (not first), above * (not last)


def sum_rows(own_x, sides_x, own_y, sides_y):
    rows = [np.einsum("ix,jy->ijxy", side, own_y) for side in sides_x]
    rows += [np.einsum("ix,jy->ijxy", own_x, side) for side in sides_y]
    for side_x in sides_x:
        for side_y in sides_y:
            corner = np.einsum("ix,jy->ijxy", side_x, side_y)
            rows.append(np.concatenate([corner, np.zeros_like(corner)]))
    return np.concatenate([row.reshape(-1, row.shape[2] * row.shape[3]) for row in rows])


def face_cells(rows_x, rows_y):
    low, x_high, y_high = range(-W, 0), range(rows_x, rows_x + W), range(rows_y, rows_y + W)
    cells = [(x, y) for x in low for y in range(rows_y)]
    cells += [(x, y) for x in x_high for y in range(rows_y)]
    cells += [(x, y) for x in range(rows_x) for y in low]
    cells += [(x, y) for x in range(rows_x) for y in y_high]
    return cells


@functools.lru_cache(None)
def tables(rows_x, rows_y, depth):
    cells = face_cells(rows_x, rows_y)
    own = [(x, y) for x in range(rows_x) for y in range(rows_y)]
    everywhere = np.array(own + cells)
    target = np.array(own)
    gap_x = np.abs(target[:, None, 0] - everywhere[None, :, 0])
    gap_y = np.abs(target[:, None, 1] - everywhere[None, :, 1])
    weights = np.array(list(STENCIL_WEIGHTS) + [0.0])
    star = np.where(gap_y == 0, weights[np.minimum(gap_x, W + 1)], 0.0)
    star = star + np.where(gap_x == 0, weights[np.minimum(gap_y, W + 1)], 0.0)
    spot = np.arange(depth)
    along = weights[np.minimum(np.abs(spot[:, None] - spot[None, :]), W + 1)]
    depth_lift = reflected(lift_matrix(depth), True, True)[:, W : W + depth].T
    kinds = ((False, False), (True, False), (False, True))
    lifts = []
    for kind_x in kinds:
        for kind_y in kinds:
            own_x, below_x, above_x = lift_by_sums(rows_x, *kind_x)
            own_y, below_y, above_y = lift_by_sums(rows_y, *kind_y)
            beside = sum_rows(own_x.T, (below_x.T, above_x.T), own_y.T, (below_y.T, above_y.T))
            lifts.append(np.concatenate([np.kron(own_x, own_y), beside.T], axis=1))
    lifts = np.stack(lifts)
    spare = -lifts.shape[2] % 128
    lifts = np.pad(lifts, ((0, 0), (0, 0), (0, spare)))
    sums = sum_rows(np.eye(rows_x), edge_sums(rows_x), np.eye(rows_y), edge_sums(rows_y))
    depth_both = np.concatenate([halves(along), halves(depth_lift)])
    return halves(star), depth_both, halves(lifts), halves(sums)


def split(values):
    high = values.astype(jnp.bfloat16)
    return high, (values - high.astype(jnp.float32)).astype(jnp.bfloat16)


def product(left, right):
    dot = functools.partial(jnp.dot, preferred_element_type=jnp.float32)
    return dot(left[0], right[0]) + (dot(left[0], right[1]) + dot(left[1], right[0]))


def choose(classes, entries, bit):
    if len(entries) == 1:
        return entries[0]
    half = len(entries) // 2
    low = choose(classes, entries[:half], bit // 2)
    high = choose(classes, entries[half:], bit // 2)
    return jnp.where((classes & bit) != 0, high, low)


def kernel(
    rows_x, rows_y,
    cells_hbm, samples_hbm, wave_hbm, table_hbm,
    now_hbm, old_hbm, classes_hbm, star_hbm, along_hbm, lift_hbm, sums_hbm,
    later, mid, code,
    cells_ref, samples_ref, wave_ref, table_ref,
    now, old, classes, star, along, lift, sums,
    courant, acc, packed, bundle, halo_a, halo_b, halo_c,
    local_sem, send_sem, recv_sem,
):
    depth = now.shape[1]
    size = rows_x * rows_y
    face_x, face_y = W * rows_y, W * rows_x
    slim_x, slim_y, corner = 2 * rows_y, 2 * rows_x, 8
    slim = 2 * slim_x + 2 * slim_y
    width = depth // PARTS
    at_x, at_y = lax.axis_index("gx"), lax.axis_index("gy")
    count_x, count_y = lax.axis_size("gx"), lax.axis_size("gy")
    shot = lax.axis_index("shot")
    low_x, high_x = at_x > 0, at_x < count_x - 1
    low_y, high_y = at_y > 0, at_y < count_y - 1
    kind_x = jnp.where(low_x, jnp.where(high_x, 0, 2), 1)
    kind_y = jnp.where(low_y, jnp.where(high_y, 0, 2), 1)

    pulls = [
        pltpu.make_async_copy(src, dst, local_sem.at[i])
        for i, (src, dst) in enumerate(
            [
                (now_hbm, now), (classes_hbm, classes), (old_hbm, old),
                (star_hbm, star), (along_hbm, along),
                (lift_hbm.at[kind_x * 3 + kind_y], lift), (sums_hbm, sums),
                (cells_hbm, cells_ref), (samples_hbm, samples_ref),
                (wave_hbm, wave_ref), (table_hbm, table_ref),
            ]
        )
    ]
    pulls[0].start()
    for pull in pulls[7:]:
        pull.start()

    steps = ((-1, low_x, low_y), (1, high_x, high_y))
    partners = [(dx, 0, has) for dx, has, _ in steps] + [(0, dy, has) for dy, _, has in steps]
    partners += [
        (dx, dy, jnp.logical_and(has_x, has_y)) for dx, has_x, _ in steps for dy, _, has_y in steps
    ]

    def device(dx, dy):
        return {"shot": shot, "gy": at_y + dy, "gx": at_x + dx}

    barrier = pltpu.get_barrier_semaphore()
    for dx, dy, has in partners:
        @pl.when(has)
        def _(dx=dx, dy=dy):
            pl.semaphore_signal(barrier, inc=1, device_id=device(dx, dy), device_id_type=MESH)

    def pack(source, where, part):
        lanes = slice(part * width, (part + 1) * width)
        for x in range(0, rows_x, 2):
            first, second = x * rows_y, (x + 1) * rows_y
            packed[where, 0, x * W : (x + 2) * W, lanes] = jnp.concatenate(
                [source[first : first + W, lanes], source[second : second + W, lanes]], axis=0
            )
            packed[where, 1, x * W : (x + 2) * W, lanes] = jnp.concatenate(
                [source[first + rows_y - W : second, lanes],
                 source[second + rows_y - W : second + rows_y, lanes]], axis=0
            )

    slots = [(0, face_x), (face_x, face_x), (2 * face_x, face_y), (2 * face_x + face_y, face_y)]
    thin = [(0, slim_x), (slim_x, slim_x), (2 * slim_x, slim_y), (2 * slim_x + slim_y, slim_y)]
    thin += [(slim + i * corner, corner) for i in range(4)]

    def layers(source, where, lanes):
        return [
            source.at[pl.ds(0, face_x), lanes],
            source.at[pl.ds(size - face_x, face_x), lanes],
            packed.at[where, 0, pl.ds(0, face_y), lanes],
            packed.at[where, 1, pl.ds(0, face_y), lanes],
        ]

    def combined(lanes):
        return [bundle.at[pl.ds(begin, length), lanes] for begin, length in thin]

    def exchange(ends, halo, places, base, part):
        lanes = pl.ds(part * width, width)
        ends = ends(lanes)
        opposite = [1, 0, 3, 2, 7, 6, 5, 4]
        sends, arrivals = [], []
        for i in range(len(ends)):
            dx, dy, has = partners[i]
            for to, found in ((opposite[i], sends), (i, arrivals)):
                start, length = places[to]
                found.append((has, pltpu.make_async_remote_copy(
                    src_ref=ends[i],
                    dst_ref=halo.at[pl.ds(start, length), lanes],
                    send_sem=send_sem.at[part, base + i],
                    recv_sem=recv_sem.at[part, base + to],
                    device_id=device(dx, dy),
                    device_id_type=MESH,
                )))
        return sends[2:] + sends[:2], arrivals

    def each(copies, act):
        for has, copy in copies:
            @pl.when(has)
            def _(copy=copy):
                act(copy)

    start = lambda copy: copy.start()
    landed = lambda copy: copy.wait_recv()
    sent = lambda copy: copy.wait_send()

    parts = range(PARTS)
    cuts = [slice(part * width, (part + 1) * width) for part in parts]
    first = [exchange(functools.partial(layers, now, 0), halo_a, slots, 0, p) for p in parts]
    second = [exchange(functools.partial(layers, mid, 1), halo_b, slots, 4, p) for p in parts]
    third = [exchange(combined, halo_c, thin, 8, p) for p in parts]

    for halo, places, lands in (
        (halo_a, slots, first[0][1]), (halo_b, slots, second[0][1]), (halo_c, thin, third[0][1])
    ):
        for i, (has, _) in enumerate(lands):
            begin, length = places[i]

            @pl.when(jnp.logical_not(has))
            def _(halo=halo, begin=begin, length=length):
                halo[begin : begin + length, :] = jnp.zeros((length, depth), jnp.float32)
    tail = slim + 4 * corner
    if halo_c.shape[0] > tail:
        halo_c[tail:, :] = jnp.zeros((halo_c.shape[0] - tail, depth), jnp.float32)

    pulls[0].wait()
    for pull in pulls[1:5]:
        pull.start()
    for part in parts:
        pack(now, 0, part)
    near_x = low_x.astype(jnp.int32) + high_x.astype(jnp.int32)
    near_y = low_y.astype(jnp.int32) + high_y.astype(jnp.int32)
    pl.semaphore_wait(barrier, near_x + near_y + near_x * near_y)
    for part in parts:
        each(first[part][0], start)
    for pull in pulls[5:7]:
        pull.start()

    for pull in pulls[7:]:
        pull.wait()
    wave_len = wave_ref.shape[0]
    all_y = rows_y * count_y
    shots = []
    for s in range(cells_ref.shape[0]):
        cell, sample = cells_ref[s], samples_ref[s]
        cell_x = lax.div(cell, all_y * depth) - at_x * rows_x
        cell_y = lax.rem(lax.div(cell, depth), all_y) - at_y * rows_y
        here = (cell_x >= 0) & (cell_x < rows_x) & (cell_y >= 0) & (cell_y < rows_y)
        spot = jnp.where(here, (cell_x * rows_y + cell_y) * depth + lax.rem(cell, depth), -1)
        following = jnp.where(sample + 1 >= wave_len, 0, sample + 1)
        shots.append((spot, wave_ref[sample], wave_ref[following]))
    entries = [table_ref[i] for i in range(table_ref.shape[0])]
    while len(entries) & (len(entries) - 1):
        entries.append(entries[-1])
    pulls[1].wait()
    pulls[2].wait()

    place = lax.broadcasted_iota(jnp.int32, (rows_y, depth), 0) * depth
    place = place + lax.broadcasted_iota(jnp.int32, (rows_y, depth), 1)

    def with_sources(base, x, step):
        for shot_at in shots:
            hit = place == shot_at[0] - x * (rows_y * depth)
            base = base + jnp.where(hit, shot_at[1 + step], 0.0)
        return base

    def first_plane(x, carry):
        rows = pl.ds(pl.multiple_of(x * rows_y, rows_y), rows_y)
        courant[rows, :] = jnp.broadcast_to(
            choose(classes[rows, :], entries, len(entries) // 2), (rows_y, depth)
        )
        old[rows, :] = with_sources(2.0 * now[rows, :] - old[rows, :], x, 0)
        return carry

    def second_plane(x, carry):
        rows = pl.ds(pl.multiple_of(x * rows_y, rows_y), rows_y)
        later[rows, :] = with_sources(2.0 * mid[rows, :] - now[rows, :], x, 1)
        return carry

    lax.fori_loop(0, rows_x, first_plane, 0)
    pulls[3].wait()
    pulls[4].wait()

    def deep(both, at, lanes):
        return product([b[:, lanes] for b in both], [along[at, lanes, lanes], along[at + 1, lanes, lanes]])

    def crossing(both, at, source, target):
        return product(
            [b[:, source] for b in both], [along[at, source, target], along[at + 1, source, target]]
        )

    seams = [
        (slice(part * width - 128, part * width), slice(part * width, part * width + 128))
        for part in range(1, PARTS)
    ]

    def inner(field):
        both = split(field[...])
        for lanes in cuts:
            own = product([star[0, :, :size], star[1, :, :size]], [b[:, lanes] for b in both])
            acc[:, lanes] = own + deep(both, 0, lanes)
        for left, right in seams:
            acc[:, left] += crossing(both, 0, right, left)
            acc[:, right] += crossing(both, 0, left, right)

    def outer(halo, lanes):
        return product([star[0, :, size:], star[1, :, size:]], split(halo[:, lanes]))

    inner(now)
    for part, lanes in enumerate(cuts):
        each(first[part][1], landed)
        mid[:, lanes] = old[:, lanes] + courant[:, lanes] * (acc[:, lanes] + outer(halo_a, lanes))
        pack(mid, 1, part)
        each(second[part][0], start)

    lax.fori_loop(0, rows_x, second_plane, 0)
    inner(mid)
    pulls[5].wait()
    pulls[6].wait()
    lifted_own = []
    for part, lanes in enumerate(cuts):
        each(second[part][1], landed)
        later[:, lanes] = later[:, lanes] + courant[:, lanes] * (
            acc[:, lanes] + outer(halo_b, lanes)
        )
        both = split(later[:, lanes])
        bundle[:, lanes] = product((sums[0], sums[1]), both)
        each(third[part][0], start)
        lifted_own.append(both)

    for lanes, both in zip(cuts, lifted_own):
        acc[:, lanes] = product([lift[0, :, :size], lift[1, :, :size]], both)
    pieces = []
    for part, lanes in enumerate(cuts):
        each(third[part][1], landed)
        beside = [lift[0, :, size:], lift[1, :, size:]]
        piece = split(acc[:, lanes] + product(beside, split(halo_c[:, lanes])))
        pieces.append(piece)
        courant[:, lanes] = product(piece, (along[2, lanes, lanes], along[3, lanes, lanes]))
        if part:
            left, right = seams[part - 1]
            over = (along[2, left, right], along[3, left, right])
            courant[:, right] += product([half[:, -128:] for half in pieces[part - 1]], over)
            back = (along[2, right, left], along[3, right, left])
            courant[:, left] += product([half[:, :128] for half in piece], back)
    lifted = courant[...]
    shrunk = jnp.maximum(jnp.abs(lifted) - DEAD_ZONE, 0.0) / QUANT_STEP
    code[...] = jnp.where(lifted < 0.0, -shrunk, shrunk)
    for sends, _ in first + second + third:
        each(sends, sent)


def put_out(*refs):
    sources, targets, sems = refs[:3], refs[3:6], refs[6]
    copies = [pltpu.make_async_copy(sources[i], targets[i], sems.at[i]) for i in range(3)]
    for copy in copies:
        copy.start()
    for copy in copies:
        copy.wait()


def shards(pressure_now, pressure_old, classes, class_table, wavelet, source_cells, samples):
    rows_x, rows_y, depth = pressure_now.shape
    size = rows_x * rows_y
    flat = (size, depth)
    star, along, lift, sums = tables(rows_x, rows_y, depth)
    halo_rows = star.shape[2] - size
    wide_rows = lift.shape[3] - size
    face_y = W * rows_x
    any_spec = pl.BlockSpec(memory_space=pl.ANY)
    hbm = pl.BlockSpec(memory_space=pltpu.HBM)
    f32 = jnp.float32
    out = jax.ShapeDtypeStruct(flat, f32)
    results = pl.pallas_call(
        functools.partial(kernel, rows_x, rows_y),
        out_shape=(out, out, out),
        in_specs=[hbm] * 11,
        out_specs=(pl.BlockSpec(memory_space=pltpu.VMEM),) * 3,
        scratch_shapes=[
            pltpu.SMEM(source_cells.shape, jnp.int32),
            pltpu.SMEM(samples.shape, jnp.int32),
            pltpu.SMEM(wavelet.shape, f32),
            pltpu.SMEM(class_table.shape, f32),
            pltpu.VMEM(flat, f32),
            pltpu.VMEM(flat, f32),
            pltpu.VMEM(flat, jnp.int32),
            pltpu.VMEM(star.shape, jnp.bfloat16),
            pltpu.VMEM(along.shape, jnp.bfloat16),
            pltpu.VMEM(lift.shape[1:], jnp.bfloat16),
            pltpu.VMEM(sums.shape, jnp.bfloat16),
            pltpu.VMEM(flat, f32),
            pltpu.VMEM(flat, f32),
            pltpu.VMEM((2, 2, face_y, depth), f32),
            pltpu.VMEM((sums.shape[1], depth), f32),
            pltpu.VMEM((halo_rows, depth), f32),
            pltpu.VMEM((halo_rows, depth), f32),
            pltpu.VMEM((wide_rows, depth), f32),
            pltpu.SemaphoreType.DMA((11,)),
            pltpu.SemaphoreType.DMA((PARTS, 16)),
            pltpu.SemaphoreType.DMA((PARTS, 16)),
        ],
        compiler_params=pltpu.CompilerParams(
            collective_id=0, has_side_effects=True, vmem_limit_bytes=VMEM_BYTES
        ),
    )(*[
        pltpu.with_memory_space_constraint(operand, pltpu.HBM)
        for operand in (
            source_cells, samples, wavelet, class_table,
            pressure_now.reshape(flat), pressure_old.reshape(flat), classes.reshape(flat),
            jnp.asarray(star), jnp.asarray(along), jnp.asarray(lift),
            jnp.asarray(sums),
        )
    ])
    results = pl.pallas_call(
        put_out,
        out_shape=(out, out, out),
        in_specs=[any_spec] * 3,
        out_specs=(hbm,) * 3,
        scratch_shapes=[pltpu.SemaphoreType.DMA((3,))],
        compiler_params=pltpu.CompilerParams(vmem_limit_bytes=VMEM_BYTES),
    )(*results)
    return tuple(result.reshape(pressure_now.shape) for result in results)


def solution(mesh):
    block = P(("shot", "gx"), "gy", None)
    return jax.shard_map(
        shards,
        mesh=mesh,
        in_specs=(block, block, block, P(), P("shot"), P("shot"), P("shot")),
        out_specs=(block, block, block),
        check_vma=False,
    )
```

```python
import functools

import jax
import jax.numpy as jnp
import ml_dtypes
import numpy as np
from jax import lax
from jax.experimental import pallas as pl
from jax.experimental.pallas import tpu as pltpu
from jax.sharding import PartitionSpec as P

STENCIL_WEIGHTS = (-205.0 / 72.0, 8.0 / 5.0, -1.0 / 5.0, 8.0 / 315.0, -1.0 / 560.0)
LIFT_ALPHA = -1.586134342
LIFT_BETA = -0.05298011854
LIFT_GAMMA = 0.8829110762
LIFT_DELTA = 0.4435068522
LIFT_SCALE = 1.149604398
DEAD_ZONE = 0.25
QUANT_STEP = 0.5
W = 4
MESH = pl.DeviceIdType.MESH
PARTS = 2
VMEM_BYTES = 32 * 1024 * 1024


def lift_matrix(size):
    field = np.eye(size + 2 * W)
    even, odd = field[0::2], field[1::2]
    odd = odd[:-1] + LIFT_ALPHA * (even[:-1] + even[1:])
    even = even[1:-1] + LIFT_BETA * (odd[:-1] + odd[1:])
    odd = odd[1:-1] + LIFT_GAMMA * (even[:-1] + even[1:])
    even = even[1:-1] + LIFT_DELTA * (odd[:-1] + odd[1:])
    out = np.zeros((size, size + 2 * W))
    out[0::2] = even / LIFT_SCALE
    out[1::2] = odd[1:] * LIFT_SCALE
    return out


def reflected(matrix, first, last):
    size = matrix.shape[0]
    out = matrix.copy()
    for step in range(1, W + 1):
        if first:
            out[:, W + step] += out[:, W - step]
            out[:, W - step] = 0.0
        if last:
            out[:, W + size - 1 - step] += out[:, W + size - 1 + step]
            out[:, W + size - 1 + step] = 0.0
    return out


def halves(matrix):
    wide = np.asarray(matrix, np.float32)
    high = wide.astype(ml_dtypes.bfloat16)
    low = (wide - high.astype(np.float32)).astype(ml_dtypes.bfloat16)
    return np.stack([high, low], axis=-3)


def edge_sums(size):
    low, high = np.zeros((2, size)), np.zeros((2, size))
    low[0, 0] = low[1, 1] = high[0, size - 1] = high[1, size - 2] = 1.0
    low[1, 2] = high[0, size - 2] = LIFT_ALPHA
    high[1, size - 3] = LIFT_BETA
    high[1, size - 4] = LIFT_BETA * LIFT_ALPHA
    high[1, size - 2] += LIFT_BETA * LIFT_ALPHA
    return low, high


def lift_by_sums(size, first, last):
    whole = lift_matrix(size)
    low, high = edge_sums(size)
    below = whole[:, :W] @ np.linalg.pinv(high[:, size - W :])
    above = whole[:, W + size :] @ np.linalg.pinv(low[:, :W])
    assert np.allclose(below @ high[:, size - W :], whole[:, :W], atol=1e-12)
    assert np.allclose(above @ low[:, :W], whole[:, W + size :], atol=1e-12)
    own = reflected(whole, first, last)[:, W : W + size]
    return own, below * (not first), above * (not last)


def sum_rows(own_x, sides_x, own_y, sides_y):
    rows = [np.einsum("ix,jy->ijxy", side, own_y) for side in sides_x]
    rows += [np.einsum("ix,jy->ijxy", own_x, side) for side in sides_y]
    for side_x in sides_x:
        for side_y in sides_y:
            corner = np.einsum("ix,jy->ijxy", side_x, side_y)
            rows.append(np.concatenate([corner, np.zeros_like(corner)]))
    return np.concatenate([row.reshape(-1, row.shape[2] * row.shape[3]) for row in rows])


def face_cells(rows_x, rows_y):
    low, x_high, y_high = range(-W, 0), range(rows_x, rows_x + W), range(rows_y, rows_y + W)
    cells = [(x, y) for x in low for y in range(rows_y)]
    cells += [(x, y) for x in x_high for y in range(rows_y)]
    cells += [(x, y) for x in range(rows_x) for y in low]
    cells += [(x, y) for x in range(rows_x) for y in y_high]
    return cells


@functools.lru_cache(None)
def tables(rows_x, rows_y, depth):
    cells = face_cells(rows_x, rows_y)
    own = [(x, y) for x in range(rows_x) for y in range(rows_y)]
    everywhere = np.array(own + cells)
    target = np.array(own)
    gap_x = np.abs(target[:, None, 0] - everywhere[None, :, 0])
    gap_y = np.abs(target[:, None, 1] - everywhere[None, :, 1])
    weights = np.array(list(STENCIL_WEIGHTS) + [0.0])
    star = np.where(gap_y == 0, weights[np.minimum(gap_x, W + 1)], 0.0)
    star = star + np.where(gap_x == 0, weights[np.minimum(gap_y, W + 1)], 0.0)
    spot = np.arange(depth)
    along = weights[np.minimum(np.abs(spot[:, None] - spot[None, :]), W + 1)]
    depth_lift = reflected(lift_matrix(depth), True, True)[:, W : W + depth].T
    kinds = ((False, False), (True, False), (False, True))
    lifts = []
    for kind_x in kinds:
        for kind_y in kinds:
            own_x, below_x, above_x = lift_by_sums(rows_x, *kind_x)
            own_y, below_y, above_y = lift_by_sums(rows_y, *kind_y)
            beside = sum_rows(own_x.T, (below_x.T, above_x.T), own_y.T, (below_y.T, above_y.T))
            lifts.append(np.concatenate([np.kron(own_x, own_y), beside.T], axis=1))
    lifts = np.stack(lifts)
    spare = -lifts.shape[2] % 128
    lifts = np.pad(lifts, ((0, 0), (0, 0), (0, spare)))
    sums = sum_rows(np.eye(rows_x), edge_sums(rows_x), np.eye(rows_y), edge_sums(rows_y))
    depth_both = np.concatenate([halves(along), halves(depth_lift)])
    return halves(star), depth_both, halves(lifts), halves(sums)


def split(values):
    high = values.astype(jnp.bfloat16)
    return high, (values - high.astype(jnp.float32)).astype(jnp.bfloat16)


def product(left, right):
    dot = functools.partial(jnp.dot, preferred_element_type=jnp.float32)
    return dot(left[0], right[0]) + (dot(left[0], right[1]) + dot(left[1], right[0]))


def choose(classes, entries, bit):
    if len(entries) == 1:
        return entries[0]
    half = len(entries) // 2
    low = choose(classes, entries[:half], bit // 2)
    high = choose(classes, entries[half:], bit // 2)
    return jnp.where((classes & bit) != 0, high, low)


def kernel(
    rows_x, rows_y,
    cells_hbm, samples_hbm, wave_hbm, table_hbm,
    now_hbm, old_hbm, classes_hbm, star_hbm, along_hbm, lift_hbm, sums_hbm,
    later, mid, code,
    cells_ref, samples_ref, wave_ref, table_ref,
    now, old, classes, star, along, lift, sums,
    courant, acc, packed, bundle, halo_a, halo_b, halo_c,
    local_sem, send_sem, recv_sem,
):
    depth = now.shape[1]
    size = rows_x * rows_y
    face_x, face_y = W * rows_y, W * rows_x
    slim_x, slim_y, corner = 2 * rows_y, 2 * rows_x, 8
    slim = 2 * slim_x + 2 * slim_y
    width = depth // PARTS
    at_x, at_y = lax.axis_index("gx"), lax.axis_index("gy")
    count_x, count_y = lax.axis_size("gx"), lax.axis_size("gy")
    shot = lax.axis_index("shot")
    low_x, high_x = at_x > 0, at_x < count_x - 1
    low_y, high_y = at_y > 0, at_y < count_y - 1
    kind_x = jnp.where(low_x, jnp.where(high_x, 0, 2), 1)
    kind_y = jnp.where(low_y, jnp.where(high_y, 0, 2), 1)

    pulls = [
        pltpu.make_async_copy(src, dst, local_sem.at[i])
        for i, (src, dst) in enumerate(
            [
                (now_hbm, now), (classes_hbm, classes), (old_hbm, old),
                (star_hbm, star), (along_hbm, along),
                (lift_hbm.at[kind_x * 3 + kind_y], lift), (sums_hbm, sums),
                (cells_hbm, cells_ref), (samples_hbm, samples_ref),
                (wave_hbm, wave_ref), (table_hbm, table_ref),
            ]
        )
    ]
    pulls[0].start()
    for pull in pulls[7:]:
        pull.start()

    steps = ((-1, low_x, low_y), (1, high_x, high_y))
    partners = [(dx, 0, has) for dx, has, _ in steps] + [(0, dy, has) for dy, _, has in steps]
    partners += [
        (dx, dy, jnp.logical_and(has_x, has_y)) for dx, has_x, _ in steps for dy, _, has_y in steps
    ]

    def device(dx, dy):
        return {"shot": shot, "gy": at_y + dy, "gx": at_x + dx}

    barrier = pltpu.get_barrier_semaphore()
    for dx, dy, has in partners:
        @pl.when(has)
        def _(dx=dx, dy=dy):
            pl.semaphore_signal(barrier, inc=1, device_id=device(dx, dy), device_id_type=MESH)

    def pack(source, where, part):
        lanes = slice(part * width, (part + 1) * width)
        for x in range(0, rows_x, 2):
            first, second = x * rows_y, (x + 1) * rows_y
            packed[where, 0, x * W : (x + 2) * W, lanes] = jnp.concatenate(
                [source[first : first + W, lanes], source[second : second + W, lanes]], axis=0
            )
            packed[where, 1, x * W : (x + 2) * W, lanes] = jnp.concatenate(
                [source[first + rows_y - W : second, lanes],
                 source[second + rows_y - W : second + rows_y, lanes]], axis=0
            )

    slots = [(0, face_x), (face_x, face_x), (2 * face_x, face_y), (2 * face_x + face_y, face_y)]
    thin = [(0, slim_x), (slim_x, slim_x), (2 * slim_x, slim_y), (2 * slim_x + slim_y, slim_y)]
    thin += [(slim + i * corner, corner) for i in range(4)]

    def layers(source, where, lanes):
        return [
            source.at[pl.ds(0, face_x), lanes],
            source.at[pl.ds(size - face_x, face_x), lanes],
            packed.at[where, 0, pl.ds(0, face_y), lanes],
            packed.at[where, 1, pl.ds(0, face_y), lanes],
        ]

    def combined(lanes):
        return [bundle.at[pl.ds(begin, length), lanes] for begin, length in thin]

    def exchange(ends, halo, places, base, part):
        lanes = pl.ds(part * width, width)
        ends = ends(lanes)
        opposite = [1, 0, 3, 2, 7, 6, 5, 4]
        sends, arrivals = [], []
        for i in range(len(ends)):
            dx, dy, has = partners[i]
            for to, found in ((opposite[i], sends), (i, arrivals)):
                start, length = places[to]
                found.append((has, pltpu.make_async_remote_copy(
                    src_ref=ends[i],
                    dst_ref=halo.at[pl.ds(start, length), lanes],
                    send_sem=send_sem.at[part, base + i],
                    recv_sem=recv_sem.at[part, base + to],
                    device_id=device(dx, dy),
                    device_id_type=MESH,
                )))
        return sends[2:] + sends[:2], arrivals

    def each(copies, act):
        for has, copy in copies:
            @pl.when(has)
            def _(copy=copy):
                act(copy)

    start = lambda copy: copy.start()
    landed = lambda copy: copy.wait_recv()
    sent = lambda copy: copy.wait_send()

    parts = range(PARTS)
    cuts = [slice(part * width, (part + 1) * width) for part in parts]
    first = [exchange(functools.partial(layers, now, 0), halo_a, slots, 0, p) for p in parts]
    second = [exchange(functools.partial(layers, mid, 1), halo_b, slots, 4, p) for p in parts]
    third = [exchange(combined, halo_c, thin, 8, p) for p in parts]

    for halo, places, lands in (
        (halo_a, slots, first[0][1]), (halo_b, slots, second[0][1]), (halo_c, thin, third[0][1])
    ):
        for i, (has, _) in enumerate(lands):
            begin, length = places[i]

            @pl.when(jnp.logical_not(has))
            def _(halo=halo, begin=begin, length=length):
                halo[begin : begin + length, :] = jnp.zeros((length, depth), jnp.float32)
    tail = slim + 4 * corner
    if halo_c.shape[0] > tail:
        halo_c[tail:, :] = jnp.zeros((halo_c.shape[0] - tail, depth), jnp.float32)

    pulls[0].wait()
    for pull in pulls[1:5]:
        pull.start()
    for part in parts:
        pack(now, 0, part)
    near_x = low_x.astype(jnp.int32) + high_x.astype(jnp.int32)
    near_y = low_y.astype(jnp.int32) + high_y.astype(jnp.int32)
    pl.semaphore_wait(barrier, near_x + near_y + near_x * near_y)
    for part in parts:
        each(first[part][0], start)
    for pull in pulls[5:7]:
        pull.start()

    for pull in pulls[7:]:
        pull.wait()
    wave_len = wave_ref.shape[0]
    all_y = rows_y * count_y
    shots = []
    for s in range(cells_ref.shape[0]):
        cell, sample = cells_ref[s], samples_ref[s]
        cell_x = lax.div(cell, all_y * depth) - at_x * rows_x
        cell_y = lax.rem(lax.div(cell, depth), all_y) - at_y * rows_y
        here = (cell_x >= 0) & (cell_x < rows_x) & (cell_y >= 0) & (cell_y < rows_y)
        spot = jnp.where(here, (cell_x * rows_y + cell_y) * depth + lax.rem(cell, depth), -1)
        following = jnp.where(sample + 1 >= wave_len, 0, sample + 1)
        shots.append((spot, wave_ref[sample], wave_ref[following]))
    entries = [table_ref[i] for i in range(table_ref.shape[0])]
    while len(entries) & (len(entries) - 1):
        entries.append(entries[-1])
    pulls[1].wait()
    pulls[2].wait()

    place = lax.broadcasted_iota(jnp.int32, (rows_y, depth), 0) * depth
    place = place + lax.broadcasted_iota(jnp.int32, (rows_y, depth), 1)

    def with_sources(base, x, step):
        for shot_at in shots:
            hit = place == shot_at[0] - x * (rows_y * depth)
            base = base + jnp.where(hit, shot_at[1 + step], 0.0)
        return base

    def first_plane(x, carry):
        rows = pl.ds(pl.multiple_of(x * rows_y, rows_y), rows_y)
        courant[rows, :] = jnp.broadcast_to(
            choose(classes[rows, :], entries, len(entries) // 2), (rows_y, depth)
        )
        old[rows, :] = with_sources(2.0 * now[rows, :] - old[rows, :], x, 0)
        return carry

    def second_plane(x, carry):
        rows = pl.ds(pl.multiple_of(x * rows_y, rows_y), rows_y)
        later[rows, :] = with_sources(2.0 * mid[rows, :] - now[rows, :], x, 1)
        return carry

    lax.fori_loop(0, rows_x, first_plane, 0)
    pulls[3].wait()
    pulls[4].wait()

    seams = [
        (slice(part * width - 128, part * width), slice(part * width, part * width + 128))
        for part in range(1, PARTS)
    ]

    def inner(field, lanes):
        both = split(field[:, lanes])
        own = product([star[0, :, :size], star[1, :, :size]], both)
        acc[:, lanes] = own + product(both, (along[0, lanes, lanes], along[1, lanes, lanes]))
        return both

    def join(halves_of):
        for part, (left, right) in enumerate(seams):
            below, above = halves_of[part], halves_of[part + 1]
            over = (along[0, left, right], along[1, left, right])
            back = (along[0, right, left], along[1, right, left])
            acc[:, right] += product([half[:, -128:] for half in below], over)
            acc[:, left] += product([half[:, :128] for half in above], back)

    def outer(halo, lanes):
        return product([star[0, :, size:], star[1, :, size:]], split(halo[:, lanes]))

    join([inner(now, lanes) for lanes in cuts])
    own_halves = []
    for part, lanes in enumerate(cuts):
        each(first[part][1], landed)
        mid[:, lanes] = old[:, lanes] + courant[:, lanes] * (acc[:, lanes] + outer(halo_a, lanes))
        pack(mid, 1, part)
        each(second[part][0], start)
        own_halves.append(inner(mid, lanes))

    lax.fori_loop(0, rows_x, second_plane, 0)
    join(own_halves)
    pulls[5].wait()
    pulls[6].wait()
    for part, lanes in enumerate(cuts):
        each(second[part][1], landed)
        later[:, lanes] = later[:, lanes] + courant[:, lanes] * (
            acc[:, lanes] + outer(halo_b, lanes)
        )
        both = split(later[:, lanes])
        bundle[:, lanes] = product((sums[0], sums[1]), both)
        each(third[part][0], start)
        acc[:, lanes] = product([lift[0, :, :size], lift[1, :, :size]], both)

    pieces = []
    for part, lanes in enumerate(cuts):
        each(third[part][1], landed)
        beside = [lift[0, :, size:], lift[1, :, size:]]
        piece = split(acc[:, lanes] + product(beside, split(halo_c[:, lanes])))
        pieces.append(piece)
        courant[:, lanes] = product(piece, (along[2, lanes, lanes], along[3, lanes, lanes]))
        if part:
            left, right = seams[part - 1]
            over = (along[2, left, right], along[3, left, right])
            courant[:, right] += product([half[:, -128:] for half in pieces[part - 1]], over)
            back = (along[2, right, left], along[3, right, left])
            courant[:, left] += product([half[:, :128] for half in piece], back)
    lifted = courant[...]
    shrunk = jnp.maximum(jnp.abs(lifted) - DEAD_ZONE, 0.0) / QUANT_STEP
    code[...] = jnp.where(lifted < 0.0, -shrunk, shrunk)
    for sends, _ in first + second + third:
        each(sends, sent)


def put_out(*refs):
    sources, targets, sems = refs[:3], refs[3:6], refs[6]
    copies = [pltpu.make_async_copy(sources[i], targets[i], sems.at[i]) for i in range(3)]
    for copy in copies:
        copy.start()
    for copy in copies:
        copy.wait()


def shards(pressure_now, pressure_old, classes, class_table, wavelet, source_cells, samples):
    rows_x, rows_y, depth = pressure_now.shape
    size = rows_x * rows_y
    flat = (size, depth)
    star, along, lift, sums = tables(rows_x, rows_y, depth)
    halo_rows = star.shape[2] - size
    wide_rows = lift.shape[3] - size
    face_y = W * rows_x
    any_spec = pl.BlockSpec(memory_space=pl.ANY)
    hbm = pl.BlockSpec(memory_space=pltpu.HBM)
    f32 = jnp.float32
    out = jax.ShapeDtypeStruct(flat, f32)
    results = pl.pallas_call(
        functools.partial(kernel, rows_x, rows_y),
        out_shape=(out, out, out),
        in_specs=[hbm] * 11,
        out_specs=(pl.BlockSpec(memory_space=pltpu.VMEM),) * 3,
        scratch_shapes=[
            pltpu.SMEM(source_cells.shape, jnp.int32),
            pltpu.SMEM(samples.shape, jnp.int32),
            pltpu.SMEM(wavelet.shape, f32),
            pltpu.SMEM(class_table.shape, f32),
            pltpu.VMEM(flat, f32),
            pltpu.VMEM(flat, f32),
            pltpu.VMEM(flat, jnp.int32),
            pltpu.VMEM(star.shape, jnp.bfloat16),
            pltpu.VMEM(along.shape, jnp.bfloat16),
            pltpu.VMEM(lift.shape[1:], jnp.bfloat16),
            pltpu.VMEM(sums.shape, jnp.bfloat16),
            pltpu.VMEM(flat, f32),
            pltpu.VMEM(flat, f32),
            pltpu.VMEM((2, 2, face_y, depth), f32),
            pltpu.VMEM((sums.shape[1], depth), f32),
            pltpu.VMEM((halo_rows, depth), f32),
            pltpu.VMEM((halo_rows, depth), f32),
            pltpu.VMEM((wide_rows, depth), f32),
            pltpu.SemaphoreType.DMA((11,)),
            pltpu.SemaphoreType.DMA((PARTS, 16)),
            pltpu.SemaphoreType.DMA((PARTS, 16)),
        ],
        compiler_params=pltpu.CompilerParams(
            collective_id=0, has_side_effects=True, vmem_limit_bytes=VMEM_BYTES
        ),
    )(*[
        pltpu.with_memory_space_constraint(operand, pltpu.HBM)
        for operand in (
            source_cells, samples, wavelet, class_table,
            pressure_now.reshape(flat), pressure_old.reshape(flat), classes.reshape(flat),
            jnp.asarray(star), jnp.asarray(along), jnp.asarray(lift),
            jnp.asarray(sums),
        )
    ])
    results = pl.pallas_call(
        put_out,
        out_shape=(out, out, out),
        in_specs=[any_spec] * 3,
        out_specs=(hbm,) * 3,
        scratch_shapes=[pltpu.SemaphoreType.DMA((3,))],
        compiler_params=pltpu.CompilerParams(vmem_limit_bytes=VMEM_BYTES),
    )(*results)
    return tuple(result.reshape(pressure_now.shape) for result in results)


def solution(mesh):
    block = P(("shot", "gx"), "gy", None)
    return jax.shard_map(
        shards,
        mesh=mesh,
        in_specs=(block, block, block, P(), P("shot"), P("shot"), P("shot")),
        out_specs=(block, block, block),
        check_vma=False,
    )
```
